128 devices in a mesh: seq: 16 (over x, y), dp: 8 (over z, core).
Axes of the slice: x: 4, y: 4, z: 4, core: 2. Of those that a mesh axis runs over, the one named last changes fastest.
Arguments:
- inputs: bfloat16 [8, 4096, 2048], P('dp', 'seq'), may hold values from -32 to 32
- w_qkv: bfloat16 [2048, 3072], replicated, may hold values from -0.088388348 to 0.088388348
- random_blocks: int32 [32, 3], replicated, may hold values from 0 to 31, as said below
- d_out: bfloat16 [8, 4096, 2048], P('dp', 'seq'), may hold values from -6 to 6
Outputs:
- attended: bfloat16 [8, 4096, 2048], P('dp', 'seq')
- d_wqkv: float32 [2048, 3072], P(('seq', 'dp'))
The draws below stay inside these ranges and needn't reach their ends.
Inputs may be any that keep to these rules, and one draw needn't show every extreme that they name: `random_blocks`: for each j, the 6 entries of rows j * 2 to (j + 1) * 2 - 1 lie in different groups of 2 consecutive blocks (entry // 2), none of them group j.
All inputs are finite; a program needn't handle non-finite values.
Results may differ from the reference program's by a relative error of at most 0.02.
Values may be sent and summed in bfloat16 or wider, within the bound.
A program may use at most 192 MiB of HBM per device.

```python
import jax
import jax.numpy as jnp
from jax import lax

D = 2048
H = 16
KVH = 4
HD = 128
BLOCK = 128
NRAND = 3
TOK_DEV = 256
SEQ_DEV = 1
BPD = 2
QBLOCKS = 32
SEQ_LEN = 4096
SEQS = 8
NSEL = 8
KVW = 1024
QKVW = 3072
N_SEQ = 16
N_DP = 8


def draw_inputs(key, part):
    key = jax.random.fold_in(key, 1)
    normal_part = jnp.clip(jax.random.normal(key, (SEQS, SEQ_LEN, D), jnp.float32), -5.0, 5.0)
    values = normal_part
    return values.astype(jnp.bfloat16)


def draw_w_qkv(key, part):
    key = jax.random.fold_in(key, 2)
    scale = D ** (-0.5)
    weights = jnp.clip(jax.random.normal(key, (D, QKVW), jnp.float32), -5.0, 5.0) * scale
    weights = jnp.clip(weights, -4.0 * scale, 4.0 * scale)
    return weights.astype(jnp.bfloat16)


def draw_random_blocks(key, part):
    key = jax.random.fold_in(key, 3)
    order_key, offset_key = jax.random.split(key)
    picks = BPD * NRAND
    groups = jnp.arange(N_SEQ, dtype=jnp.int32)[:, None]
    others = jnp.arange(N_SEQ - 1, dtype=jnp.int32)[None, :]
    owners = (groups + 1 + others) % N_SEQ
    scores = jax.random.randint(order_key, (N_SEQ, N_SEQ - 1), 0, 1 << 20, jnp.int32) * N_SEQ + others + 1
    forced = (groups == 0) & (owners == N_SEQ - 1) | (groups == N_SEQ - 1) & (owners == 0)
    scores = jnp.where(forced, 0, scores)
    ranking = jnp.argsort(scores, axis=1, stable=True)
    chosen = jnp.take_along_axis(owners, ranking[:, :picks], axis=1)
    offsets = jax.random.randint(offset_key, (N_SEQ, picks), 0, BPD, jnp.int32)
    offsets = offsets.at[0, 0].set(BPD - 1).at[N_SEQ - 1, 0].set(0)
    return (chosen * BPD + offsets).reshape(QBLOCKS, NRAND).astype(jnp.int32)


def block_scale(own_key, dims, cuts, low, top_value):
    factor_of, own = 1.0, jax.random.fold_in(own_key, 6)
    for dim, parts in cuts:
        heights = jnp.exp(jax.random.uniform(jax.random.fold_in(own, dim), (parts,), jnp.float32, low / len(cuts), top_value / len(cuts)))
        factor_of = factor_of * jnp.repeat(heights, dims[dim] // parts).reshape([-1 if axis == dim else 1 for axis in range(len(dims))])
    return factor_of


def gaussian(own_key, extent, deviation, bound, pieces=(), kind=jnp.bfloat16):
    factor_of = block_scale(own_key, extent, pieces, -0.22, 0.18) if pieces else 1.0
    result = jax.random.normal(own_key, extent, jnp.float32) * deviation * factor_of
    return jnp.minimum(jnp.maximum(result, -bound), bound).astype(kind)


def setup_inputs(seed: int = 0) -> dict:
    splits = jax.random.split(jax.random.key(seed), 5)
    inputs = draw_inputs(jax.random.fold_in(splits[4], 71), 0)
    w_qkv = draw_w_qkv(jax.random.fold_in(splits[4], 71), 0)
    random_blocks = draw_random_blocks(jax.random.fold_in(splits[4], 71), 0)
    d_out = gaussian(splits[3], (SEQS, SEQ_LEN, H * HD), 1.0, 6.0, ((0, 8), (1, 16)))
    return dict(inputs=inputs, w_qkv=w_qkv, random_blocks=random_blocks, d_out=d_out)


def attend(q_block, key_tiles, dout_block):
    group = H // KVH
    scale = HD ** -0.5
    queries = q_block.astype(jnp.float32).reshape(BLOCK, KVH, group, HD)
    keys = key_tiles[:, :KVH * HD].astype(jnp.float32).reshape(-1, KVH, HD)
    values = key_tiles[:, KVH * HD:].astype(jnp.float32).reshape(-1, KVH, HD)
    scores = jnp.einsum('qgrd,kgd->grqk', queries, keys) * scale
    peak = jnp.max(scores, axis=-1, keepdims=True)
    expos = jnp.exp(scores - peak)
    probs = expos / jnp.sum(expos, axis=-1, keepdims=True)
    weights = lax.optimization_barrier(probs.astype(jnp.bfloat16)).astype(jnp.float32)
    attended = jnp.einsum('grqk,kgd->qgrd', weights, values).reshape(BLOCK, H * HD).astype(jnp.bfloat16)
    grads = dout_block.astype(jnp.float32).reshape(BLOCK, KVH, group, HD)
    dprob = jnp.einsum('qgrd,kgd->grqk', grads, values)
    dscore = probs * (dprob - jnp.sum(probs * dprob, axis=-1, keepdims=True))
    dweights = lax.optimization_barrier((dscore * scale).astype(jnp.bfloat16)).astype(jnp.float32)
    d_query = jnp.einsum('grqk,kgd->qgrd', dweights, keys).reshape(BLOCK, H * HD).astype(jnp.bfloat16)
    d_key = jnp.einsum('grqk,qgrd->kgd', dweights, queries).reshape(-1, KVH * HD)
    d_value = jnp.einsum('grqk,qgrd->kgd', weights, grads).reshape(-1, KVH * HD)
    return attended, d_query, jnp.concatenate([d_key, d_value], axis=-1)


def reference(inputs, w_qkv, random_blocks, d_out):
    projected = jnp.dot(inputs.reshape(-1, D), w_qkv, preferred_element_type=jnp.float32).astype(jnp.bfloat16)
    projected = projected.reshape(SEQS, SEQ_LEN, QKVW)
    blocks = jnp.arange(QBLOCKS, dtype=jnp.int32)
    window = jnp.stack([(blocks - 1) % QBLOCKS, blocks, (blocks + 1) % QBLOCKS], axis=1)
    global_ids = jnp.broadcast_to(jnp.array([0, 1], dtype=jnp.int32), (QBLOCKS, 2))
    key_lists = jnp.concatenate([window, global_ids, random_blocks.astype(jnp.int32)], axis=1)

    def one_sequence(pair_args):
        seq_proj, seq_dout = pair_args
        kv_tiles = seq_proj[:, H * HD:].reshape(QBLOCKS, BLOCK, KVW)
        query_tiles = seq_proj[:, :H * HD].reshape(QBLOCKS, BLOCK, H * HD)
        dout_tiles = seq_dout.reshape(QBLOCKS, BLOCK, H * HD)

        def one_block(block):
            chosen = kv_tiles[key_lists[block]].reshape(NSEL * BLOCK, KVW)
            return attend(query_tiles[block], chosen, dout_tiles[block])

        outputs, d_query, terms = lax.map(one_block, blocks)
        terms = terms.reshape(QBLOCKS, NSEL, BLOCK, KVW)
        near_terms = terms[:, :5]
        far_terms = lax.optimization_barrier(terms[:, 5:].astype(jnp.bfloat16)).astype(jnp.float32)
        summed = jnp.zeros((QBLOCKS, BLOCK, KVW), jnp.float32)
        summed = summed.at[key_lists[:, :5]].add(near_terms)
        summed = summed.at[key_lists[:, 5:]].add(far_terms)
        d_qkv = jnp.concatenate([d_query.reshape(SEQ_LEN, H * HD),
                                 summed.astype(jnp.bfloat16).reshape(SEQ_LEN, KVW)], axis=1)
        return outputs.reshape(SEQ_LEN, H * HD), d_qkv

    attended, d_qkv = lax.map(one_sequence, (projected, d_out))
    in_groups = inputs.reshape(N_DP, SEQ_DEV, N_SEQ, TOK_DEV, D).transpose(0, 2, 1, 3, 4)
    in_groups = in_groups.reshape(N_DP * N_SEQ, SEQ_DEV * TOK_DEV, D)
    g_groups = d_qkv.reshape(N_DP, SEQ_DEV, N_SEQ, TOK_DEV, QKVW).transpose(0, 2, 1, 3, 4)
    g_groups = g_groups.reshape(N_DP * N_SEQ, SEQ_DEV * TOK_DEV, QKVW)

    def add_group(running, pair_args):
        in_part, g_part = pair_args
        partial_sum = jnp.dot(in_part.T, g_part, preferred_element_type=jnp.float32)
        partial_sum = lax.optimization_barrier(partial_sum.astype(jnp.bfloat16)).astype(jnp.float32)
        return running + partial_sum, None

    d_wqkv, _ = lax.scan(add_group, jnp.zeros((D, QKVW), jnp.float32), (in_groups, g_groups))
    return attended, d_wqkv
```

```python
import functools

import jax
import jax.numpy as jnp
from jax import lax
from jax.experimental import pallas as pl
from jax.experimental.pallas import tpu as pltpu
from jax.sharding import PartitionSpec as P

RING = 4
TOK = 256
BLOCK = 128
D = 2048
HD = 128
GROUP = 4
QW = GROUP * HD
GW = QW + 2 * HD
QBLOCKS = 32
NRAND = 3
SCALE = HD ** -0.5
EXP2_SCALE = SCALE * 1.4426950408889634
BF = jnp.bfloat16
F32 = jnp.float32
MESH = pl.DeviceIdType.MESH
VM = pl.BlockSpec(memory_space=pltpu.VMEM)
HBM = pl.BlockSpec(memory_space=pl.ANY)


def places():
    s, d = lax.axis_index("seq"), lax.axis_index("dp")
    x, y, z, c = s // RING, s % RING, d // 2, d % 2
    return x + c * (y - x), y + c * (x - y), z, c


def shard_of(c, q, r):
    return q * (RING - 3 * c) + r * (1 + 3 * c)


def turn(i, steps):
    return lax.rem(i + steps, RING)


def wait_in(ref, sem):
    pltpu.make_async_copy(ref, ref, sem).wait()


def gather_kernel(x_ref, w_ref, g_ref, xt_out, q_out, g_out, kv_out,
                  xbuf, wbuf, xtbuf, qbuf, kvbuf,
                  local_sem, x_send, x_recv, g_send, g_recv, kv_send, kv_recv, out_sem):
    q, r, z, c = places()

    def peer(q_, r_):
        return (shard_of(c, q_, r_), z * 2 + c)

    rs = [turn(r, k) for k in (1, 3, 2)]
    qs = [turn(q, k) for k in (1, 3, 2)]
    locals_ = [
        pltpu.make_async_copy(x_ref, xbuf.at[r], local_sem.at[0]),
        pltpu.make_async_copy(w_ref.at[:, pl.ds(pl.multiple_of(r * QW, QW), QW)], wbuf.at[:, 0:QW], local_sem.at[1]),
        pltpu.make_async_copy(w_ref.at[:, pl.ds(pl.multiple_of(2048 + r * HD, HD), HD)],
                              wbuf.at[:, QW:QW + HD], local_sem.at[2]),
        pltpu.make_async_copy(w_ref.at[:, pl.ds(pl.multiple_of(2560 + r * HD, HD), HD)],
                              wbuf.at[:, QW + HD:GW], local_sem.at[3]),
        pltpu.make_async_copy(g_ref.at[:, pl.ds(pl.multiple_of(r * QW, QW), QW)], g_out.at[r], local_sem.at[4]),
    ]
    for copy in locals_:
        copy.start()

    barrier = pltpu.get_barrier_semaphore()
    for k in range(3):
        pl.semaphore_signal(barrier, inc=1, device_id=peer(q, rs[k]), device_id_type=MESH)
        pl.semaphore_signal(barrier, inc=1, device_id=peer(qs[k], r), device_id_type=MESH)
    pl.semaphore_wait(barrier, 6)

    def remote(src, dst, send, recv, to):
        copy = pltpu.make_async_remote_copy(src_ref=src, dst_ref=dst, send_sem=send, recv_sem=recv,
                                            device_id=to, device_id_type=MESH)
        copy.start()
        return copy

    up, down, far = rs
    halves = (pl.ds(0, BLOCK), pl.ds(BLOCK, BLOCK))
    sent = []
    for n, (half, to) in enumerate(((0, up), (1, down), (1, up), (0, down))):
        sent.append(remote(x_ref.at[halves[half]], xbuf.at[r, halves[half]], x_send.at[n], x_recv.at[n], peer(q, to)))

    outs = []

    def project(step, j):
        for part in range(3):
            cols = slice(part * 256, (part + 1) * 256)
            got = jnp.dot(xbuf[j], wbuf[:, cols], preferred_element_type=F32).astype(BF)
            if part < 2:
                qbuf[j, :, cols] = got
            else:
                kvbuf[j] = got
        slot = kv_out.at[q * RING + j]
        for k in range(3):
            sent.append(remote(kvbuf.at[j], slot, kv_send.at[step * 3 + k], kv_recv.at[step * 3 + k], peer(qs[k], r)))
        outs.append(pltpu.make_async_copy(kvbuf.at[j], slot, out_sem.at[step * 2]))
        outs[-1].start()
        outs.append(pltpu.make_async_copy(qbuf.at[j], q_out.at[j], out_sem.at[step * 2 + 1]))
        outs[-1].start()

    def transpose(j):
        turned = xbuf[j].T.reshape(RING, RING, RING, 32, TOK)
        xtbuf[:, :, :, :, pl.ds(pl.multiple_of(j * TOK, TOK), TOK)] = turned

    for copy in locals_[:4]:
        copy.wait()
    project(0, r)
    transpose(r)
    wait_in(xbuf.at[down, halves[0]], x_recv.at[0])
    sent.append(remote(xbuf.at[down, halves[0]], xbuf.at[down, halves[0]], x_send.at[4], x_recv.at[4], peer(q, up)))
    wait_in(xbuf.at[up, halves[1]], x_recv.at[1])
    sent.append(remote(xbuf.at[up, halves[1]], xbuf.at[up, halves[1]], x_send.at[5], x_recv.at[5], peer(q, down)))
    wait_in(xbuf.at[down, halves[1]], x_recv.at[2])
    project(1, down)
    wait_in(xbuf.at[up, halves[0]], x_recv.at[3])
    project(2, up)
    for k in range(3):
        sent.append(remote(g_ref.at[:, pl.ds(pl.multiple_of(rs[k] * QW, QW), QW)], g_out.at[r],
                           g_send.at[k], g_recv.at[k], peer(q, rs[k])))
    transpose(down)
    transpose(up)
    wait_in(xbuf.at[far, halves[0]], x_recv.at[4])
    wait_in(xbuf.at[far, halves[1]], x_recv.at[5])
    project(3, far)
    transpose(far)
    outs.append(pltpu.make_async_copy(xtbuf, xt_out, out_sem.at[8]))
    outs[-1].start()

    for step, j in enumerate((r, down, up, far)):
        for k, source in enumerate((qs[1], qs[0], qs[2])):
            wait_in(kv_out.at[source * RING + j], kv_recv.at[step * 3 + k])
    for k, source in enumerate((down, up, far)):
        wait_in(g_out.at[source], g_recv.at[k])
    for copy in sent:
        copy.wait_send()
    for copy in outs + locals_[4:]:
        copy.wait()


def gather(inputs, w_qkv, d_out):
    return pl.pallas_call(
        gather_kernel,
        out_shape=[
            jax.ShapeDtypeStruct((RING, RING, RING, 32, RING * TOK), BF),
            jax.ShapeDtypeStruct((RING, TOK, QW), BF),
            jax.ShapeDtypeStruct((RING, TOK, QW), BF),
            jax.ShapeDtypeStruct((RING * RING, TOK, 2 * HD), BF),
        ],
        in_specs=[HBM] * 3,
        out_specs=[HBM] * 4,
        scratch_shapes=[
            pltpu.VMEM((RING, TOK, D), BF),
            pltpu.VMEM((D, GW), BF),
            pltpu.VMEM((RING, RING, RING, 32, RING * TOK), BF),
            pltpu.VMEM((RING, TOK, QW), BF),
            pltpu.VMEM((RING, TOK, 2 * HD), BF),
            pltpu.SemaphoreType.DMA((5,)),
            pltpu.SemaphoreType.DMA((6,)),
            pltpu.SemaphoreType.DMA((6,)),
            pltpu.SemaphoreType.DMA((3,)),
            pltpu.SemaphoreType.DMA((3,)),
            pltpu.SemaphoreType.DMA((12,)),
            pltpu.SemaphoreType.DMA((12,)),
            pltpu.SemaphoreType.DMA((9,)),
        ],
        compiler_params=pltpu.CompilerParams(collective_id=1, has_side_effects=True, vmem_limit_bytes=40 * 2**20),
        cost_estimate=pl.CostEstimate(flops=2 * 1024 * D * GW, bytes_accessed=20 * 2**20, transcendentals=0),
        name="gather_project",
    )(inputs, w_qkv, d_out)


def attend_kernel(rb, q_ref, g_ref, kv_ref, att_ref, dq_ref, dkv_ref, kcat, acc):
    q, r, z, c = places()
    i = pl.program_id(0)
    b = shard_of(c, q, i // 2) * 2 + i % 2

    @pl.when(i == 0)
    def _():
        acc[...] = jnp.zeros_like(acc)

    listed = [lax.rem(b + QBLOCKS - 1, QBLOCKS), b, lax.rem(b + 1, QBLOCKS), jnp.int32(0), jnp.int32(1)]
    listed += [rb[b, n] for n in range(NRAND)]

    def slot(n):
        s = n // 2
        return (s + c * ((s % RING) * RING + s // RING - s)) * 2 + n % 2

    ids = [slot(n) for n in listed]
    for l, n in enumerate(ids):
        kcat[pl.ds(l * BLOCK, BLOCK), :] = kv_ref[n]
    keys, values = kcat[:, :HD], kcat[:, HD:]
    heads = [slice(h * HD, (h + 1) * HD) for h in range(GROUP)]
    queries = jnp.concatenate([q_ref[0, :, h] for h in heads], axis=0)
    grads = jnp.concatenate([g_ref[0, :, h] for h in heads], axis=0)
    nt = (((1,), (1,)), ((), ()))
    scores = lax.dot_general(keys, queries, nt, preferred_element_type=F32)
    peak = jnp.max(scores, axis=0, keepdims=True)
    expos = jnp.exp2((scores - peak) * EXP2_SCALE)
    probs = expos * (1.0 / jnp.sum(expos, axis=0, keepdims=True))
    weights = probs.astype(BF)
    dprob = lax.dot_general(values, grads, nt, preferred_element_type=F32)
    attended = jnp.dot(values.T, weights, preferred_element_type=F32)
    mean = jnp.sum(probs * dprob, axis=0, keepdims=True)
    dweights = (probs * (dprob - mean) * SCALE).astype(BF)
    d_query = jnp.dot(keys.T, dweights, preferred_element_type=F32)
    for h in heads:
        att_ref[0, :, h] = attended[:, h].T.astype(BF)
        dq_ref[0, :, h] = d_query[:, h].T.astype(BF)
    d_key = jnp.dot(dweights, queries, preferred_element_type=F32)
    d_value = jnp.dot(weights, grads, preferred_element_type=F32)
    for l, n in enumerate(ids):
        rows = slice(l * BLOCK, (l + 1) * BLOCK)
        acc[n, :, 0:HD] += d_key[rows]
        acc[n, :, HD:] += d_value[rows]

    @pl.when(i == 7)
    def _():
        dkv_ref[...] = acc[...].astype(BF)


def attend(random_blocks, queries, grads, kv):
    whole = lambda i, *_: (0, 0, 0)
    block = pl.BlockSpec((1, BLOCK, QW), lambda i, *_: (i, 0, 0))
    return pl.pallas_call(
        attend_kernel,
        grid_spec=pltpu.PrefetchScalarGridSpec(
            num_scalar_prefetch=1,
            grid=(2 * RING,),
            in_specs=[block, block, pl.BlockSpec((QBLOCKS, BLOCK, 2 * HD), whole)],
            out_specs=[block, block, pl.BlockSpec((QBLOCKS, BLOCK, 2 * HD), whole)],
            scratch_shapes=[pltpu.VMEM((8 * BLOCK, 2 * HD), BF), pltpu.VMEM((QBLOCKS, BLOCK, 2 * HD), F32)],
        ),
        out_shape=[
            jax.ShapeDtypeStruct((2 * RING, BLOCK, QW), BF),
            jax.ShapeDtypeStruct((2 * RING, BLOCK, QW), BF),
            jax.ShapeDtypeStruct((QBLOCKS, BLOCK, 2 * HD), BF),
        ],
        compiler_params=pltpu.CompilerParams(vmem_limit_bytes=48 * 2**20),
        cost_estimate=pl.CostEstimate(flops=12 * 2**29, bytes_accessed=8 * 2**20, transcendentals=2**22),
        name="attend",
    )(random_blocks, queries.reshape(2 * RING, BLOCK, QW), grads.reshape(2 * RING, BLOCK, QW),
      kv.reshape(QBLOCKS, BLOCK, 2 * HD))


def reduce_kernel(xt_ref, dq_ref, dkv_ref, att_ref, att_out, dw_out,
                  xt, dq, dkv_own, dkv_in, dkv, zs, zin, qs_, qin, ks, kin, kzs, kzin, fs, fin,
                  local_sem, dkv_send, dkv_recv, att_send, att_recv, z_send, z_recv, q_send, q_recv,
                  k_send, k_recv, kz_send, kz_recv, f_send, f_recv):
    q, r, z, c = places()
    order = (1, 3, 2)
    rs = [turn(r, k) for k in order]
    qs = [turn(q, k) for k in order]
    zz = [turn(z, k) for k in order]
    back = (1, 0, 2)

    def peer(q_, r_, z_):
        return (shard_of(c, q_, r_), z_ * 2 + c)

    @pl.when(c == 0)
    def _():
        for i in range(RING):
            pltpu.make_async_copy(xt_ref.at[i, :, :], xt.at[i], local_sem.at[0]).start()

    @pl.when(c == 1)
    def _():
        for i in range(RING):
            pltpu.make_async_copy(xt_ref.at[:, i, :], xt.at[i], local_sem.at[0]).start()

    load_dq = pltpu.make_async_copy(dq_ref, dq, local_sem.at[1])
    load_dq.start()
    load_dkv = pltpu.make_async_copy(dkv_ref.at[pl.ds(q * RING, RING)], dkv_own, local_sem.at[2])
    load_dkv.start()
    own_att = pltpu.make_async_copy(att_ref.at[r], att_out.at[:, pl.ds(pl.multiple_of(r * QW, QW), QW)], local_sem.at[3])
    own_att.start()

    barrier = pltpu.get_barrier_semaphore()
    met = [peer(q, rs[k], z) for k in range(3)] + [peer(qs[k], r, z) for k in range(3)]
    met += [peer(q, r, zz[k]) for k in range(3)]
    met += [(shard_of(c, q, turn(r, k)), z * 2 + 1 - c) for k in range(RING)]
    met += [(shard_of(c, turn(q, k), r), z * 2 + 1 - c) for k in range(RING)]
    for device in met:
        pl.semaphore_signal(barrier, inc=1, device_id=device, device_id_type=MESH)
    pl.semaphore_wait(barrier, len(met))

    sent = []

    def remote(src, dst, send, recv, to):
        copy = pltpu.make_async_remote_copy(src_ref=src, dst_ref=dst, send_sem=send, recv_sem=recv,
                                            device_id=to, device_id_type=MESH)
        copy.start()
        sent.append(copy)

    for k in range(3):
        remote(dkv_ref.at[pl.ds(qs[k] * RING, RING)], dkv_in.at[k], dkv_send.at[k], dkv_recv.at[k], peer(qs[k], r, z))
    for k in range(3):
        remote(att_ref.at[rs[k]], att_out.at[:, pl.ds(pl.multiple_of(r * QW, QW), QW)],
               att_send.at[k], att_recv.at[k], peer(q, rs[k], z))

    load_dq.wait()
    wait_in(xt, local_sem.at[0])
    dq_all = dq[...].reshape(RING * TOK, QW)

    def rows_of(z_, q_):
        return xt[q_, :, z_].reshape(RING * 32, RING * TOK)

    for k in (2, 0, 1):
        for q_ in range(RING):
            zs[k, q_] = jnp.dot(rows_of(zz[k], q_), dq_all, preferred_element_type=F32).astype(BF)
        remote(zs.at[k], zin.at[k], z_send.at[k], z_recv.at[k], peer(q, r, zz[k]))
    own_z = [jnp.dot(rows_of(z, q_), dq_all, preferred_element_type=F32) for q_ in range(RING)]
    for q_ in range(RING):
        zs[3, q_] = own_z[q_].astype(BF)

    load_dkv.wait()
    for k in range(3):
        wait_in(dkv_in.at[k], dkv_recv.at[k])
    total = dkv_own[...].astype(F32)
    for k in range(3):
        total += dkv_in[k].astype(F32)
    dkv[...] = total.astype(BF)
    dkv_all = dkv[...].reshape(RING * TOK, 2 * HD)
    for k in (2, 0, 1):
        for z_ in range(RING):
            ks[k, z_] = jnp.dot(rows_of(z_, qs[k]), dkv_all, preferred_element_type=F32).astype(BF)
        remote(ks.at[k], kin.at[k], k_send.at[k], k_recv.at[k], peer(qs[k], r, z))
    for z_ in range(RING):
        ks[3, z_] = jnp.dot(rows_of(z_, q), dkv_all, preferred_element_type=F32).astype(BF)
    for k in range(3):
        wait_in(kin.at[k], k_recv.at[k])
    for k in range(3):
        got = ks[3, zz[k]].astype(F32)
        for n in range(3):
            got += kin[n, zz[k]].astype(F32)
        kzs[k] = got.astype(BF)
        remote(kzs.at[k], kzin.at[k], kz_send.at[k], kz_recv.at[k], peer(q, r, zz[k]))

    for k in range(3):
        wait_in(zin.at[k], z_recv.at[k])
    for k in range(3):
        got = zs[3, qs[k]].astype(F32)
        for n in range(3):
            got += zin[n, qs[k]].astype(F32)
        qs_[k] = got.astype(BF)
        remote(qs_.at[k], qin.at[k], q_send.at[k], q_recv.at[k], peer(qs[k], r, z))
    own_q = zs[3, q].astype(F32)
    own_k = ks[3, z].astype(F32)
    for n in range(3):
        own_q += zin[n, q].astype(F32)
        own_k += kin[n, z].astype(F32)
    for k in range(3):
        wait_in(qin.at[k], q_recv.at[k])
        wait_in(kzin.at[k], kz_recv.at[k])
    for k in range(3):
        own_q += qin[k].astype(F32)
        own_k += kzin[k].astype(F32)
    fs[:, :, :, 0:QW] = own_q.astype(BF).reshape(RING, 2, 16, QW)
    fs[:, :, :, QW:GW] = own_k.astype(BF).reshape(RING, 2, 16, 2 * HD)

    for k in range(RING):
        to = turn(r, k)
        if k:
            remote(fs.at[to, c], fin.at[0, k], f_send.at[k], f_recv.at[k], (shard_of(c, q, to), z * 2 + c))
        remote(fs.at[to, 1 - c], fin.at[1, k], f_send.at[RING + k], f_recv.at[RING + k],
               (shard_of(c, q, to), z * 2 + 1 - c))
    fin[0, 0] = fs[r, c]
    for k in range(RING):
        if k:
            wait_in(fin.at[0, k], f_recv.at[k])
        wait_in(fin.at[1, k], f_recv.at[RING + k])
    for g in range(RING):
        mine = fin[0, lax.rem(r + RING - g, RING)].astype(F32)
        other = fin[1, lax.rem(q + RING - g, RING)].astype(F32)
        got = mine + other
        dw_out[:, g * QW:(g + 1) * QW] = got[:, 0:QW]
        dw_out[:, 2048 + g * HD:2048 + (g + 1) * HD] = got[:, QW:QW + HD]
        dw_out[:, 2560 + g * HD:2560 + (g + 1) * HD] = got[:, QW + HD:GW]

    for k in range(3):
        wait_in(att_out.at[:, pl.ds(pl.multiple_of(rs[back[k]] * QW, QW), QW)], att_recv.at[k])
    for copy in sent:
        copy.wait_send()
    own_att.wait()


def reduce(xt, d_query, d_kv, attended):
    dma = pltpu.SemaphoreType.DMA
    return pl.pallas_call(
        reduce_kernel,
        out_shape=[jax.ShapeDtypeStruct((TOK, D), BF), jax.ShapeDtypeStruct((16, RING * GW), F32)],
        in_specs=[HBM] * 4,
        out_specs=[HBM, VM],
        scratch_shapes=[
            pltpu.VMEM((RING, RING, RING, 32, RING * TOK), BF),
            pltpu.VMEM((RING, TOK, QW), BF),
            pltpu.VMEM((RING, TOK, 2 * HD), BF),
            pltpu.VMEM((3, RING, TOK, 2 * HD), BF),
            pltpu.VMEM((RING, TOK, 2 * HD), BF),
            pltpu.VMEM((4, RING, 128, QW), BF),
            pltpu.VMEM((3, RING, 128, QW), BF),
            pltpu.VMEM((3, 128, QW), BF),
            pltpu.VMEM((3, 128, QW), BF),
            pltpu.VMEM((4, RING, 128, 2 * HD), BF),
            pltpu.VMEM((3, RING, 128, 2 * HD), BF),
            pltpu.VMEM((3, 128, 2 * HD), BF),
            pltpu.VMEM((3, 128, 2 * HD), BF),
            pltpu.VMEM((RING, 2, 16, GW), BF),
            pltpu.VMEM((2, RING, 16, GW), BF),
            dma((4,)), dma((3,)), dma((3,)), dma((3,)), dma((3,)), dma((3,)), dma((3,)), dma((3,)), dma((3,)),
            dma((3,)), dma((3,)), dma((3,)), dma((3,)), dma((8,)), dma((8,)),
        ],
        compiler_params=pltpu.CompilerParams(collective_id=2, has_side_effects=True, vmem_limit_bytes=40 * 2**20),
        cost_estimate=pl.CostEstimate(flops=2 * 1024 * D * GW, bytes_accessed=12 * 2**20, transcendentals=0),
        name="weight_gradient",
    )(xt, d_query.reshape(RING, TOK, QW), d_kv.reshape(RING * RING, TOK, 2 * HD), attended.reshape(RING, TOK, QW))


def body(inputs, w_qkv, random_blocks, d_out):
    xt, queries, grads, kv = gather(inputs[0], w_qkv, d_out[0])
    attended, d_query, d_kv = attend(random_blocks, queries, grads, kv)
    attended, d_wqkv = reduce(xt, d_query, d_kv, attended)
    return attended[None], d_wqkv


def solution(mesh):
    return jax.shard_map(
        body,
        mesh=mesh,
        in_specs=(P("dp", "seq", None), P(), P(), P("dp", "seq", None)),
        out_specs=(P("dp", "seq", None), P(("seq", "dp"), None)),
        check_vma=False,
    )
```

```python
import jax
import jax.numpy as jnp
from jax import lax
from jax.experimental import pallas as pl
from jax.experimental.pallas import tpu as pltpu
from jax.sharding import PartitionSpec as P

RING = 4
TOK = 256
BLOCK = 128
D = 2048
HD = 128
GROUP = 4
QW = GROUP * HD
KV = 2 * HD
GW = QW + KV
QBLOCKS = 32
NRAND = 3
LOCAL = 2 * RING
PICKS = LOCAL * NRAND
SCALE = HD ** -0.5
EXP2_SCALE = SCALE * 1.4426950408889634
BF = jnp.bfloat16
F32 = jnp.float32
MESH = pl.DeviceIdType.MESH


def places():
    s, d = lax.axis_index("seq"), lax.axis_index("dp")
    x, y, z, c = s // RING, s % RING, d // 2, d % 2
    return x + c * (y - x), y + c * (x - y), z, c


def shard_of(c, q, r):
    return q * (RING - 3 * c) + r * (1 + 3 * c)


def turn(i, steps):
    return lax.rem(i + steps, RING)


def wait_in(ref, sem):
    pltpu.make_async_copy(ref, ref, sem).wait()


def dot(a, b):
    return jnp.dot(a, b, preferred_element_type=F32)


def kernel(rb, x_ref, w_ref, g_ref, att_out, dw_out,
           xall, wkv, wq, kvown, qown, kvall, qall, gall, attb, dqb, near, terms, kcat, ids, prev, last,
           xt, dkvs, dkv_in, dkv, zs, zin, qs_, qin, ks, kin, kzs, kzin, fs, fin,
           local_sem, wq_sem, a_send, a_recv, kv_send, kv_recv, q_send, q_recv, g_send, g_recv, x_send, x_recv,
           dkv_send, dkv_recv, att_send, att_recv, z_send, z_recv, dq_send, dq_recv, k_send, k_recv, kz_send, kz_recv,
           f_send, f_recv):
    q, r, z, c = places()
    rs = [turn(r, k) for k in (1, 3, 2)]
    qs = [turn(q, k) for k in (1, 3, 2)]
    zz = [turn(z, k) for k in (1, 3, 2)]
    up, down, far = rs
    r_from = (down, up, far)
    q_from = (qs[1], qs[0], qs[2])

    def peer(q_, r_, z_):
        return (shard_of(c, q_, r_), z_ * 2 + c)

    load_x = pltpu.make_async_copy(x_ref, xall.at[r], local_sem.at[0])
    load_x.start()
    load_wkv = pltpu.make_async_copy(w_ref.at[:, pl.ds(RING * QW, RING * KV)], wkv, local_sem.at[1])
    load_wkv.start()
    load_g = pltpu.make_async_copy(g_ref.at[:, pl.ds(pl.multiple_of(r * QW, QW), QW)], gall.at[r], local_sem.at[2])
    load_wq = [pltpu.make_async_copy(w_ref.at[:, pl.ds(pl.multiple_of(to * QW, QW), QW)], wq.at[k], wq_sem.at[k])
               for k, to in enumerate((up, down, far, r))]

    barrier = pltpu.get_barrier_semaphore()
    met = [peer(q, rs[k], z) for k in range(3)] + [peer(qs[k], r, z) for k in range(3)]
    met += [peer(q, r, zz[k]) for k in range(3)]
    met += [(shard_of(c, q, turn(r, k)), z * 2 + 1 - c) for k in range(RING)]
    met += [(shard_of(c, turn(q, k), r), z * 2 + 1 - c) for k in range(RING)]
    for device in met:
        pl.semaphore_signal(barrier, inc=1, device_id=device, device_id_type=MESH)

    sent = []

    def remote(src, dst, send, recv, to):
        copy = pltpu.make_async_remote_copy(src_ref=src, dst_ref=dst, send_sem=send, recv_sem=recv,
                                            device_id=to, device_id_type=MESH)
        sent.append(copy)
        return copy

    load_x.wait()
    load_wkv.wait()
    for copy in load_wq:
        copy.start()
    load_g.start()
    x_own = xall[r]
    for part in range(4):
        got = dot(x_own, wkv[:, part * 256:(part + 1) * 256]).astype(BF)
        cols = slice(0, HD) if part < 2 else slice(HD, KV)
        for n in range(2):
            kvown[part % 2 * 2 + n, :, :, cols] = got[:, n * HD:(n + 1) * HD].reshape(2, BLOCK, HD)
    pl.semaphore_wait(barrier, len(met))

    def slot(j):
        return kvall.at[pl.ds((q * RING + j) * 2, 2)]

    for k in range(3):
        remote(kvown.at[rs[k]], slot(r), a_send.at[k], a_recv.at[k], peer(q, rs[k], z)).start()

    def pass_on(step, src, j):
        for k in range(3):
            remote(src, slot(j), kv_send.at[step * 3 + k], kv_recv.at[step * 3 + k], peer(qs[k], r, z)).start()

    pass_on(0, kvown.at[r], r)
    kvall[pl.ds((q * RING + r) * 2, 2)] = kvown[r]

    for k in range(4):
        load_wq[k].wait()
        for part in range(2):
            cols = slice(part * 256, (part + 1) * 256)
            got = dot(x_own, wq[k, :, cols]).astype(BF)
            if k < 3:
                qown[k, :, cols] = got
            else:
                qall[r, :, cols] = got

    for k, j in enumerate(r_from):
        wait_in(slot(j), a_recv.at[k])
        pass_on(k + 1, slot(j), j)

    def step_j(step):
        return turn(r, jnp.where(step == 0, 0, jnp.where(step == 1, 3, step - 1)))

    def place_of(n):
        s = n // 2
        return (s + c * ((s % RING) * RING + s // RING - s)) * 2 + n % 2

    def fill_ids(i, _):
        b = shard_of(c, q, step_j(i // 2)) * 2 + i % 2
        for n in range(NRAND):
            ids[i * NRAND + n] = place_of(rb[b, n])
        return 0

    lax.fori_loop(0, LOCAL, fill_ids, 0)

    def fill_prev(k, _):
        mine = ids[k]
        got = jnp.int32(PICKS)
        for n in range(PICKS):
            got = jnp.where((ids[n] == mine) & (n < k), n, got)
        prev[k] = got
        return 0

    lax.fori_loop(0, PICKS, fill_prev, 0)

    def fill_last(n, _):
        got = jnp.int32(PICKS)
        for k in range(PICKS):
            got = jnp.where(ids[k] == n, k, got)
        last[n] = got
        return 0

    lax.fori_loop(0, QBLOCKS, fill_last, 0)
    near[...] = jnp.zeros_like(near)
    terms[PICKS] = jnp.zeros((BLOCK, KV), F32)

    def transpose(j):
        turned = xall[j].T.reshape(RING * RING, RING, 32, TOK)
        xt[:, :, :, pl.ds(pl.multiple_of(j * TOK, TOK), TOK)] = turned

    transpose(r)

    q_copies, g_copies = [], []
    for k in range(3):
        q_copies.append(remote(qown.at[k], qall.at[r], q_send.at[k], q_recv.at[k], peer(q, rs[k], z)))
        g_copies.append(remote(g_ref.at[:, pl.ds(pl.multiple_of(rs[k] * QW, QW), QW)], gall.at[r],
                               g_send.at[k], g_recv.at[k], peer(q, rs[k], z)))
    halves = (pl.ds(0, BLOCK), pl.ds(BLOCK, BLOCK))
    x_copies = [remote(xall.at[r, halves[half]], xall.at[r, halves[half]], x_send.at[n], x_recv.at[n], peer(q, to, z))
                for n, (half, to) in enumerate(((0, up), (1, down), (1, up), (0, down)))]
    x_on = [remote(xall.at[down, halves[0]], xall.at[down, halves[0]], x_send.at[4], x_recv.at[4], peer(q, up, z)),
            remote(xall.at[up, halves[1]], xall.at[up, halves[1]], x_send.at[5], x_recv.at[5], peer(q, down, z))]

    for step, j in enumerate((r, down, up, far)):
        for k in range(3):
            wait_in(kvall.at[pl.ds((q_from[k] * RING + j) * 2, 2)], kv_recv.at[step * 3 + k])
    load_g.wait()
    for k in range(3):
        q_copies[k].start()
        g_copies[k].start()

    def attend(i, _):
        @pl.when(i == 1)
        def _():
            for copy in x_copies:
                copy.start()

        for k in range(3):
            @pl.when(i == 2 * k + 2)
            def _():
                wait_in(qall.at[r_from[k]], q_recv.at[k])
                wait_in(gall.at[r_from[k]], g_recv.at[k])

        @pl.when(i == 7)
        def _():
            wait_in(xall.at[down, halves[0]], x_recv.at[0])
            x_on[0].start()
            wait_in(xall.at[up, halves[1]], x_recv.at[1])
            x_on[1].start()

        j = step_j(i // 2)
        b = shard_of(c, q, j) * 2 + i % 2
        rows = pl.ds(pl.multiple_of((i % 2) * BLOCK, BLOCK), BLOCK)
        near_ids = [place_of(n) for n in (lax.rem(b + QBLOCKS - 1, QBLOCKS), b, lax.rem(b + 1, QBLOCKS),
                                          jnp.int32(0), jnp.int32(1))]
        listed = near_ids + [ids[i * NRAND + n] for n in range(NRAND)]
        for l, n in enumerate(listed):
            kcat[pl.ds(l * BLOCK, BLOCK), :] = kvall[n]
        keys, values = kcat[:, :HD], kcat[:, HD:]
        heads = [slice(h * HD, (h + 1) * HD) for h in range(GROUP)]
        queries = jnp.concatenate([qall[j, rows, h] for h in heads], axis=0)
        grads = jnp.concatenate([gall[j, rows, h] for h in heads], axis=0)
        nt = (((1,), (1,)), ((), ()))
        scores = lax.dot_general(keys, queries, nt, preferred_element_type=F32)
        peak = jnp.max(scores, axis=0, keepdims=True)
        expos = jnp.exp2((scores - peak) * EXP2_SCALE)
        probs = expos * (1.0 / jnp.sum(expos, axis=0, keepdims=True))
        weights = probs.astype(BF)
        dprob = lax.dot_general(values, grads, nt, preferred_element_type=F32)
        attended = dot(values.T, weights)
        mean = jnp.sum(probs * dprob, axis=0, keepdims=True)
        dweights = (probs * (dprob - mean) * SCALE).astype(BF)
        d_query = dot(keys.T, dweights)
        for h in heads:
            attb[j, rows, h] = attended[:, h].T.astype(BF)
            dqb[j, rows, h] = d_query[:, h].T.astype(BF)
        d_key = dot(dweights, queries)
        d_value = dot(weights, grads)
        for l, n in enumerate(near_ids):
            at = slice(l * BLOCK, (l + 1) * BLOCK)
            near[n, :, 0:HD] += d_key[at]
            near[n, :, HD:] += d_value[at]
        for l in range(NRAND):
            at = slice((5 + l) * BLOCK, (6 + l) * BLOCK)
            k = i * NRAND + l
            before = terms[prev[k]]
            terms[k, :, 0:HD] = before[:, 0:HD] + d_key[at]
            terms[k, :, HD:] = before[:, HD:] + d_value[at]
        return 0

    lax.fori_loop(0, LOCAL, attend, 0)

    for k in range(3):
        def gather_terms(n, _):
            at = qs[k] * LOCAL + n
            dkvs[at] = (near[at] + terms[last[at]]).astype(BF)
            return 0

        lax.fori_loop(0, LOCAL, gather_terms, 0)
        remote(dkvs.at[pl.ds(qs[k] * LOCAL, LOCAL)], dkv_in.at[k], dkv_send.at[k], dkv_recv.at[k],
               peer(qs[k], r, z)).start()

    wait_in(xall.at[down, halves[1]], x_recv.at[2])
    transpose(down)
    wait_in(xall.at[up, halves[0]], x_recv.at[3])
    transpose(up)
    wait_in(xall.at[far, halves[0]], x_recv.at[4])
    wait_in(xall.at[far, halves[1]], x_recv.at[5])
    transpose(far)
    dq_all = dqb[...].reshape(RING * TOK, QW)

    def rows_of(z_, q_):
        return jnp.concatenate([xt[shard_of(c, q_, n), z_] for n in range(RING)], axis=0)

    for k in (2, 0, 1):
        for q_ in range(RING):
            zs[k, q_] = dot(rows_of(zz[k], q_), dq_all).astype(BF)
        remote(zs.at[k], zin.at[k], z_send.at[k], z_recv.at[k], peer(q, r, zz[k])).start()
    for q_ in range(RING):
        zs[3, q_] = dot(rows_of(z, q_), dq_all).astype(BF)

    for k in range(3):
        wait_in(dkv_in.at[k], dkv_recv.at[k])

    def add_terms(n, _):
        at = q * LOCAL + n
        got = near[at] + terms[last[at]]
        for k in range(3):
            got += dkv_in[k, n].astype(F32)
        dkv[n] = got.astype(BF)
        return 0

    lax.fori_loop(0, LOCAL, add_terms, 0)
    dkv_all = dkv[...].reshape(RING * TOK, KV)
    for k in (2, 0, 1):
        for z_ in range(RING):
            ks[k, z_] = dot(rows_of(z_, qs[k]), dkv_all).astype(BF)
        remote(ks.at[k], kin.at[k], k_send.at[k], k_recv.at[k], peer(qs[k], r, z)).start()
    for k in range(3):
        remote(attb.at[rs[k]], att_out.at[:, pl.ds(pl.multiple_of(r * QW, QW), QW)],
               att_send.at[k], att_recv.at[k], peer(q, rs[k], z)).start()
    own_att = pltpu.make_async_copy(attb.at[r], att_out.at[:, pl.ds(pl.multiple_of(r * QW, QW), QW)], local_sem.at[3])
    own_att.start()
    for z_ in range(RING):
        ks[3, z_] = dot(rows_of(z_, q), dkv_all).astype(BF)
    for k in range(3):
        wait_in(kin.at[k], k_recv.at[k])
    for k in range(3):
        got = ks[3, zz[k]].astype(F32)
        for n in range(3):
            got += kin[n, zz[k]].astype(F32)
        kzs[k] = got.astype(BF)
        remote(kzs.at[k], kzin.at[k], kz_send.at[k], kz_recv.at[k], peer(q, r, zz[k])).start()

    for k in range(3):
        wait_in(zin.at[k], z_recv.at[k])
    for k in range(3):
        got = zs[3, qs[k]].astype(F32)
        for n in range(3):
            got += zin[n, qs[k]].astype(F32)
        qs_[k] = got.astype(BF)
        remote(qs_.at[k], qin.at[k], dq_send.at[k], dq_recv.at[k], peer(qs[k], r, z)).start()
    own_q = zs[3, q].astype(F32)
    own_k = ks[3, z].astype(F32)
    for n in range(3):
        own_q += zin[n, q].astype(F32)
        own_k += kin[n, z].astype(F32)
    for k in range(3):
        wait_in(qin.at[k], dq_recv.at[k])
        wait_in(kzin.at[k], kz_recv.at[k])
    for k in range(3):
        own_q += qin[k].astype(F32)
        own_k += kzin[k].astype(F32)
    fs[:, :, :, 0:QW] = own_q.astype(BF).reshape(RING, 2, 16, QW)
    fs[:, :, :, QW:GW] = own_k.astype(BF).reshape(RING, 2, 16, KV)

    for k in range(RING):
        to = turn(r, k)
        if k:
            remote(fs.at[to, c], fin.at[0, k], f_send.at[k], f_recv.at[k], (shard_of(c, q, to), z * 2 + c)).start()
        remote(fs.at[to, 1 - c], fin.at[1, k], f_send.at[RING + k], f_recv.at[RING + k],
               (shard_of(c, q, to), z * 2 + 1 - c)).start()
    fin[0, 0] = fs[r, c]
    for k in range(RING):
        if k:
            wait_in(fin.at[0, k], f_recv.at[k])
        wait_in(fin.at[1, k], f_recv.at[RING + k])
    for g in range(RING):
        mine = fin[0, lax.rem(r + RING - g, RING)].astype(F32)
        other = fin[1, lax.rem(q + RING - g, RING)].astype(F32)
        got = mine + other
        dw_out[:, g * QW:(g + 1) * QW] = got[:, 0:QW]
        dw_out[:, 2048 + g * HD:2048 + (g + 1) * HD] = got[:, QW:QW + HD]
        dw_out[:, 2560 + g * HD:2560 + (g + 1) * HD] = got[:, QW + HD:GW]

    for k in range(3):
        wait_in(att_out.at[:, pl.ds(pl.multiple_of(r_from[k] * QW, QW), QW)], att_recv.at[k])
    for copy in sent:
        copy.wait_send()
    own_att.wait()


def body(inputs, w_qkv, random_blocks, d_out):
    dma = pltpu.SemaphoreType.DMA
    vm = pltpu.VMEM
    hbm = pl.BlockSpec(memory_space=pl.ANY)
    attended, d_wqkv = pl.pallas_call(
        kernel,
        out_shape=[jax.ShapeDtypeStruct((TOK, D), BF), jax.ShapeDtypeStruct((16, RING * GW), F32)],
        in_specs=[pl.BlockSpec(memory_space=pltpu.SMEM), hbm, hbm, hbm],
        out_specs=[hbm, pl.BlockSpec(memory_space=pltpu.VMEM)],
        scratch_shapes=[
            vm((RING, TOK, D), BF),
            vm((D, RING * KV), BF),
            vm((RING, D, QW), BF),
            vm((RING, 2, BLOCK, KV), BF),
            vm((3, TOK, QW), BF),
            vm((QBLOCKS, BLOCK, KV), BF),
            vm((RING, TOK, QW), BF),
            vm((RING, TOK, QW), BF),
            vm((RING, TOK, QW), BF),
            vm((RING, TOK, QW), BF),
            vm((QBLOCKS, BLOCK, KV), F32),
            vm((PICKS + 1, BLOCK, KV), F32),
            vm((8 * BLOCK, KV), BF),
            pltpu.SMEM((PICKS,), jnp.int32),
            pltpu.SMEM((PICKS,), jnp.int32),
            pltpu.SMEM((QBLOCKS,), jnp.int32),
            vm((RING * RING, RING, 32, RING * TOK), BF),
            vm((QBLOCKS, BLOCK, KV), BF),
            vm((3, LOCAL, BLOCK, KV), BF),
            vm((LOCAL, BLOCK, KV), BF),
            vm((4, RING, 128, QW), BF),
            vm((3, RING, 128, QW), BF),
            vm((3, 128, QW), BF),
            vm((3, 128, QW), BF),
            vm((4, RING, 128, KV), BF),
            vm((3, RING, 128, KV), BF),
            vm((3, 128, KV), BF),
            vm((3, 128, KV), BF),
            vm((RING, 2, 16, GW), BF),
            vm((2, RING, 16, GW), BF),
            dma((4,)), dma((4,)),
            dma((3,)), dma((3,)), dma((12,)), dma((12,)), dma((3,)), dma((3,)), dma((3,)), dma((3,)), dma((6,)), dma((6,)),
            dma((3,)), dma((3,)), dma((3,)), dma((3,)), dma((3,)), dma((3,)), dma((3,)), dma((3,)), dma((3,)), dma((3,)),
            dma((3,)), dma((3,)), dma((8,)), dma((8,)),
        ],
        compiler_params=pltpu.CompilerParams(collective_id=1, has_side_effects=True, vmem_limit_bytes=62 * 2**20),
        cost_estimate=pl.CostEstimate(flops=13 * 10**9, bytes_accessed=20 * 2**20, transcendentals=2**22),
        name="attention_weight_gradient",
    )(random_blocks, inputs[0], w_qkv, d_out[0])
    return attended[None], d_wqkv


def solution(mesh):
    return jax.shard_map(
        body,
        mesh=mesh,
        in_specs=(P("dp", "seq", None), P(), P(), P("dp", "seq", None)),
        out_specs=(P("dp", "seq", None), P(("seq", "dp"), None)),
        check_vma=False,
    )
```

```python
import jax
import jax.numpy as jnp
from jax import lax
from jax.experimental import pallas as pl
from jax.experimental.pallas import tpu as pltpu
from jax.sharding import PartitionSpec as P

RING = 4
TOK = 256
BLOCK = 128
D = 2048
HD = 128
GROUP = 4
QW = GROUP * HD
KV = 2 * HD
GW = QW + KV
QBLOCKS = 32
NRAND = 3
LOCAL = 2 * RING
PICKS = LOCAL * NRAND
SCALE = HD ** -0.5
EXP2_SCALE = SCALE * 1.4426950408889634
BF = jnp.bfloat16
F32 = jnp.float32
MESH = pl.DeviceIdType.MESH


def places():
    s, d = lax.axis_index("seq"), lax.axis_index("dp")
    x, y, z, c = s // RING, s % RING, d // 2, d % 2
    return x + c * (y - x), y + c * (x - y), z, c


def shard_of(c, q, r):
    return q * (RING - 3 * c) + r * (1 + 3 * c)


def turn(i, steps):
    return lax.rem(i + steps, RING)


def wait_in(ref, sem):
    pltpu.make_async_copy(ref, ref, sem).wait()


def dot(a, b):
    return jnp.dot(a, b, preferred_element_type=F32)


def kernel(rb, x_ref, w_ref, g_ref, att_out, fin_out,
           xall, wkv, wq, kvown, qown, kvall, qall, gall, attb, dqb, near, terms, kcat, ids, prev, last,
           xt, dkvs, dkv_far, dkv_in, dkv, zs, z_far, zin, qs_, qin, ks, kin, kzs, kzin, fs, fin,
           local_sem, wq_sem, a_send, a_recv, kv_send, kv_recv, q_send, q_recv, g_send, g_recv, x_send, x_recv,
           dkv_send, dkv_recv, att_send, att_recv, z_send, z_recv, dq_send, dq_recv, k_send, k_recv, kz_send, kz_recv,
           f_send, f_recv):
    q, r, z, c = places()
    rs = [turn(r, k) for k in (1, 3, 2)]
    qs = [turn(q, k) for k in (1, 3, 2)]
    zz = [turn(z, k) for k in (1, 3, 2)]
    up, down, far = rs
    r_from = (down, up, far)
    q_from = (qs[1], qs[0], qs[2])

    def peer(q_, r_, z_):
        return (shard_of(c, q_, r_), z_ * 2 + c)

    load_x = pltpu.make_async_copy(x_ref, xall.at[r], local_sem.at[0])
    load_x.start()
    load_wkv = pltpu.make_async_copy(w_ref.at[:, pl.ds(RING * QW, RING * KV)], wkv, local_sem.at[1])
    load_wkv.start()
    load_g = pltpu.make_async_copy(g_ref.at[:, pl.ds(pl.multiple_of(r * QW, QW), QW)], gall.at[r], local_sem.at[2])
    load_wq = [pltpu.make_async_copy(w_ref.at[:, pl.ds(pl.multiple_of(to * QW, QW), QW)], wq.at[k], wq_sem.at[k])
               for k, to in enumerate((up, down, far, r))]

    barrier = pltpu.get_barrier_semaphore()
    met = [peer(q, rs[k], z) for k in range(3)] + [peer(qs[k], r, z) for k in range(3)]
    met += [peer(q, r, zz[k]) for k in range(3)]
    met += [(shard_of(c, q, turn(r, k)), z * 2 + 1 - c) for k in range(RING)]
    met += [(shard_of(c, turn(q, k), r), z * 2 + 1 - c) for k in range(RING)]
    for device in met:
        pl.semaphore_signal(barrier, inc=1, device_id=device, device_id_type=MESH)

    sent = []

    def remote(src, dst, send, recv, to):
        copy = pltpu.make_async_remote_copy(src_ref=src, dst_ref=dst, send_sem=send, recv_sem=recv,
                                            device_id=to, device_id_type=MESH)
        sent.append(copy)
        return copy

    load_x.wait()
    load_wkv.wait()
    for copy in load_wq:
        copy.start()
    load_g.start()
    x_own = xall[r]
    for part in range(4):
        got = dot(x_own, wkv[:, part * 256:(part + 1) * 256]).astype(BF)
        cols = slice(0, HD) if part < 2 else slice(HD, KV)
        for n in range(2):
            kvown[part % 2 * 2 + n, :, :, cols] = got[:, n * HD:(n + 1) * HD].reshape(2, BLOCK, HD)
    pl.semaphore_wait(barrier, len(met))

    def slot(j):
        return kvall.at[pl.ds((q * RING + j) * 2, 2)]

    for k in range(3):
        remote(kvown.at[rs[k]], slot(r), a_send.at[k], a_recv.at[k], peer(q, rs[k], z)).start()

    def pass_on(step, src, j):
        for k in range(2):
            remote(src, slot(j), kv_send.at[step * 4 + k], kv_recv.at[step * 4 + k], peer(qs[k], r, z)).start()

    def pass_on_block(step, j):
        for k in range(2):
            whole = kvall.at[pl.ds((q_from[k] * RING + j) * 2, 2)]
            wait_in(whole, kv_recv.at[step * 4 + k])
            block = kvall.at[pl.ds((q_from[k] * RING + j) * 2 + k, 1)]
            remote(block, block, kv_send.at[step * 4 + 2 + k], kv_recv.at[step * 4 + 2 + k], peer(qs[k], r, z)).start()

    def project_queries(k):
        load_wq[k].wait()
        for part in range(2):
            cols = slice(part * 256, (part + 1) * 256)
            got = dot(x_own, wq[k, :, cols]).astype(BF)
            if k < 3:
                qown[k, :, cols] = got
            else:
                qall[r, :, cols] = got

    pass_on(0, kvown.at[r], r)
    kvall[pl.ds((q * RING + r) * 2, 2)] = kvown[r]
    project_queries(0)
    for k in range(2):
        wait_in(slot(r_from[k]), a_recv.at[k])
        pass_on(k + 1, slot(r_from[k]), r_from[k])
    project_queries(1)
    wait_in(slot(far), a_recv.at[2])
    pass_on(3, slot(far), far)
    pass_on_block(0, r)
    project_queries(2)
    project_queries(3)

    def step_j(step):
        return turn(r, jnp.where(step == 0, 0, jnp.where(step == 1, 3, step - 1)))

    def place_of(n):
        s = n // 2
        return (s + c * ((s % RING) * RING + s // RING - s)) * 2 + n % 2

    def fill_ids(i, _):
        b = shard_of(c, q, step_j(i // 2)) * 2 + i % 2
        for n in range(NRAND):
            ids[i * NRAND + n] = place_of(rb[b, n])
        return 0

    lax.fori_loop(0, LOCAL, fill_ids, 0)

    def fill_prev(k, _):
        mine = ids[k]
        got = jnp.int32(PICKS)
        for n in range(PICKS):
            got = jnp.where((ids[n] == mine) & (n < k), n, got)
        prev[k] = got
        return 0

    lax.fori_loop(0, PICKS, fill_prev, 0)

    def fill_last(n, _):
        got = jnp.int32(PICKS)
        for k in range(PICKS):
            got = jnp.where(ids[k] == n, k, got)
        last[n] = got
        return 0

    lax.fori_loop(0, QBLOCKS, fill_last, 0)
    pass_on_block(1, down)
    pass_on_block(2, up)
    pass_on_block(3, far)
    near[...] = jnp.zeros_like(near)
    terms[PICKS] = jnp.zeros((BLOCK, KV), F32)

    def transpose(j):
        turned = xall[j].T.reshape(RING * RING, RING, 32, TOK)
        xt[:, :, :, pl.ds(pl.multiple_of(j * TOK, TOK), TOK)] = turned

    transpose(r)

    q_copies, g_copies = [], []
    for k in range(3):
        q_copies.append(remote(qown.at[k], qall.at[r], q_send.at[k], q_recv.at[k], peer(q, rs[k], z)))
        g_copies.append(remote(g_ref.at[:, pl.ds(pl.multiple_of(rs[k] * QW, QW), QW)], gall.at[r],
                               g_send.at[k], g_recv.at[k], peer(q, rs[k], z)))
    halves = (pl.ds(0, BLOCK), pl.ds(BLOCK, BLOCK))
    x_copies = [remote(xall.at[r, halves[half]], xall.at[r, halves[half]], x_send.at[n], x_recv.at[n], peer(q, to, z))
                for n, (half, to) in enumerate(((0, up), (1, down), (1, up), (0, down)))]
    x_on = [remote(xall.at[down, halves[0]], xall.at[down, halves[0]], x_send.at[4], x_recv.at[4], peer(q, up, z)),
            remote(xall.at[up, halves[1]], xall.at[up, halves[1]], x_send.at[5], x_recv.at[5], peer(q, down, z))]

    for step, j in enumerate((r, down, up, far)):
        for k in range(2):
            wait_in(kvall.at[pl.ds((qs[2] * RING + j) * 2 + k, 1)], kv_recv.at[step * 4 + 2 + k])
    load_g.wait()
    for k in range(3):
        q_copies[k].start()
        g_copies[k].start()

    def attend(i, _):
        @pl.when(i == 1)
        def _():
            x_copies[0].start()
            x_copies[1].start()

        @pl.when(i == 3)
        def _():
            x_copies[2].start()
            x_copies[3].start()

        for k in range(3):
            @pl.when(i == 2 * k + 2)
            def _():
                wait_in(qall.at[r_from[k]], q_recv.at[k])
                wait_in(gall.at[r_from[k]], g_recv.at[k])

        @pl.when(i == 6)
        def _():
            wait_in(xall.at[down, halves[0]], x_recv.at[0])
            x_on[0].start()
            wait_in(xall.at[up, halves[1]], x_recv.at[1])
            x_on[1].start()

        j = step_j(i // 2)
        b = shard_of(c, q, j) * 2 + i % 2
        rows = pl.ds(pl.multiple_of((i % 2) * BLOCK, BLOCK), BLOCK)
        near_ids = [place_of(n) for n in (lax.rem(b + QBLOCKS - 1, QBLOCKS), b, lax.rem(b + 1, QBLOCKS),
                                          jnp.int32(0), jnp.int32(1))]
        listed = near_ids + [ids[i * NRAND + n] for n in range(NRAND)]
        for l, n in enumerate(listed):
            kcat[pl.ds(l * BLOCK, BLOCK), :] = kvall[n]
        keys, values = kcat[:, :HD], kcat[:, HD:]
        heads = [slice(h * HD, (h + 1) * HD) for h in range(GROUP)]
        queries = jnp.concatenate([qall[j, rows, h] for h in heads], axis=0)
        grads = jnp.concatenate([gall[j, rows, h] for h in heads], axis=0)
        nt = (((1,), (1,)), ((), ()))
        scores = lax.dot_general(keys, queries, nt, preferred_element_type=F32)
        peak = jnp.max(scores, axis=0, keepdims=True)
        expos = jnp.exp2((scores - peak) * EXP2_SCALE)
        probs = expos * (1.0 / jnp.sum(expos, axis=0, keepdims=True))
        weights = probs.astype(BF)
        dprob = lax.dot_general(values, grads, nt, preferred_element_type=F32)
        attended = dot(values.T, weights)
        mean = jnp.sum(probs * dprob, axis=0, keepdims=True)
        dweights = (probs * (dprob - mean)).astype(BF)
        d_query = dot(keys.T, dweights) * SCALE
        for h in heads:
            attb[j, rows, h] = attended[:, h].T.astype(BF)
            dqb[j, rows, h] = d_query[:, h].T.astype(BF)
        d_key = dot(dweights, queries) * SCALE
        d_value = dot(weights, grads)
        for l, n in enumerate(near_ids):
            at = slice(l * BLOCK, (l + 1) * BLOCK)
            near[n, :, 0:HD] += d_key[at]
            near[n, :, HD:] += d_value[at]
        for l in range(NRAND):
            at = slice((5 + l) * BLOCK, (6 + l) * BLOCK)
            k = i * NRAND + l
            before = terms[prev[k]]
            terms[k, :, 0:HD] = before[:, 0:HD] + d_key[at]
            terms[k, :, HD:] = before[:, HD:] + d_value[at]
        return 0

    lax.fori_loop(0, LOCAL, attend, 0)

    def ring_far(chunk, landed, send, recv, to):
        for k in range(2):
            remote(chunk(2, k), landed.at[k], send.at[k], recv.at[k], to[k]).start()

    def ring_free(chunk, arrived, send, recv, to):
        for k in range(2):
            remote(chunk(k, 1 - k), arrived(k, 1 - k), send.at[2 + k], recv.at[2 + k], to[k]).start()

    def ring_rest(chunk, landed, arrived, send, recv, to):
        for k in range(2):
            wait_in(landed.at[k], recv.at[k])
            chunk(k, k)[...] = (chunk(k, k)[...].astype(F32) + landed[k].astype(F32)).astype(BF)
            remote(chunk(k, k), arrived(k, k), send.at[4 + k], recv.at[4 + k], to[k]).start()

    def ring_wait(arrived, recv):
        for k in range(2):
            wait_in(arrived(k, 1 - k), recv.at[2 + k])
            wait_in(arrived(k, k), recv.at[4 + k])

    def dkv_chunk(k, half):
        return dkvs.at[pl.ds(qs[k] * LOCAL + half * RING, RING)]

    def dkv_arrived(k, half):
        return dkv_in.at[k, pl.ds(half * RING, RING)]

    q_peers = [peer(qs[k], r, z) for k in range(2)]
    z_peers = [peer(q, r, zz[k]) for k in range(2)]

    def gather_terms(k):
        def one(n, _):
            at = qs[k] * LOCAL + n
            dkvs[at] = (near[at] + terms[last[at]]).astype(BF)
            return 0

        lax.fori_loop(0, LOCAL, one, 0)

    gather_terms(2)
    ring_far(dkv_chunk, dkv_far, dkv_send, dkv_recv, q_peers)
    gather_terms(0)
    gather_terms(1)
    ring_free(dkv_chunk, dkv_arrived, dkv_send, dkv_recv, q_peers)

    wait_in(xall.at[down, halves[1]], x_recv.at[2])
    transpose(down)
    wait_in(xall.at[up, halves[0]], x_recv.at[3])
    transpose(up)
    ring_rest(dkv_chunk, dkv_far, dkv_arrived, dkv_send, dkv_recv, q_peers)
    wait_in(xall.at[far, halves[0]], x_recv.at[4])
    wait_in(xall.at[far, halves[1]], x_recv.at[5])
    transpose(far)
    dq_all = dqb[...].reshape(RING * TOK, QW)

    def rows_of(z_, q_):
        return jnp.concatenate([xt[shard_of(c, q_, n), z_] for n in range(RING)], axis=0)

    def z_chunk(k, half):
        return zs.at[k, pl.ds(half * 2, 2)]

    def z_arrived(k, half):
        return zin.at[k, pl.ds(half * 2, 2)]

    def z_product(k, z_):
        for q_ in range(RING):
            zs[k, q_] = dot(rows_of(z_, q_), dq_all).astype(BF)

    z_product(2, zz[2])
    ring_far(z_chunk, z_far, z_send, z_recv, z_peers)
    z_product(0, zz[0])
    z_product(1, zz[1])
    ring_free(z_chunk, z_arrived, z_send, z_recv, z_peers)
    z_product(3, z)

    ring_wait(dkv_arrived, dkv_recv)

    def add_terms(n, _):
        at = q * LOCAL + n
        got = near[at] + terms[last[at]]
        for k in range(2):
            got += dkv_in[k, n].astype(F32)
        dkv[n] = got.astype(BF)
        return 0

    lax.fori_loop(0, LOCAL, add_terms, 0)
    ring_rest(z_chunk, z_far, z_arrived, z_send, z_recv, z_peers)
    dkv_all = dkv[...].reshape(RING * TOK, KV)
    for k in (2, 0, 1):
        for z_ in range(RING):
            ks[k, z_] = dot(rows_of(z_, qs[k]), dkv_all).astype(BF)
        remote(ks.at[k], kin.at[k], k_send.at[k], k_recv.at[k], peer(qs[k], r, z)).start()
    for k in range(3):
        remote(attb.at[rs[k]], att_out.at[r],
               att_send.at[k], att_recv.at[k], peer(q, rs[k], z)).start()
    own_att = pltpu.make_async_copy(attb.at[r], att_out.at[r], local_sem.at[3])
    own_att.start()
    for z_ in range(RING):
        ks[3, z_] = dot(rows_of(z_, q), dkv_all).astype(BF)
    for k in range(3):
        wait_in(kin.at[k], k_recv.at[k])
    for k in range(3):
        got = ks[3, zz[k]].astype(F32)
        for n in range(3):
            got += kin[n, zz[k]].astype(F32)
        kzs[k] = got.astype(BF)
        remote(kzs.at[k], kzin.at[k], kz_send.at[k], kz_recv.at[k], peer(q, r, zz[k])).start()

    ring_wait(z_arrived, z_recv)
    for k in range(3):
        got = zs[3, qs[k]].astype(F32)
        for n in range(2):
            got += zin[n, qs[k]].astype(F32)
        qs_[k] = got.astype(BF)
        remote(qs_.at[k], qin.at[k], dq_send.at[k], dq_recv.at[k], peer(qs[k], r, z)).start()
    own_q = zs[3, q].astype(F32)
    own_k = ks[3, z].astype(F32)
    for n in range(3):
        own_k += kin[n, z].astype(F32)
    for n in range(2):
        own_q += zin[n, q].astype(F32)
    for k in range(3):
        wait_in(qin.at[k], dq_recv.at[k])
        wait_in(kzin.at[k], kz_recv.at[k])
    for k in range(3):
        own_q += qin[k].astype(F32)
        own_k += kzin[k].astype(F32)
    fs[:, :, :, 0:QW] = own_q.astype(BF).reshape(RING, 2, 16, QW)
    fs[:, :, :, QW:GW] = own_k.astype(BF).reshape(RING, 2, 16, KV)

    for k in range(RING):
        to = turn(r, k)
        if k:
            remote(fs.at[to, c], fin.at[0, k], f_send.at[k], f_recv.at[k], (shard_of(c, q, to), z * 2 + c)).start()
        remote(fs.at[to, 1 - c], fin.at[1, k], f_send.at[RING + k], f_recv.at[RING + k],
               (shard_of(c, q, to), z * 2 + 1 - c)).start()
    fin[0, 0] = fs[r, c]
    for k in range(RING):
        if k:
            wait_in(fin.at[0, k], f_recv.at[k])
        wait_in(fin.at[1, k], f_recv.at[RING + k])
    for g in range(RING):
        fin_out[0, g] = fin[0, lax.rem(r + RING - g, RING)]
        fin_out[1, g] = fin[1, lax.rem(q + RING - g, RING)]

    for k in range(3):
        wait_in(att_out.at[r_from[k]], att_recv.at[k])
    for copy in sent:
        copy.wait_send()
    own_att.wait()


def results_kernel(att_ref, sums_ref, att_out, dw_out, sem):
    copies = [pltpu.make_async_copy(att_ref.at[g], att_out.at[:, pl.ds(g * QW, QW)], sem.at[g]) for g in range(RING)]
    for copy in copies:
        copy.start()
    for g in range(RING):
        got = sums_ref[0, g].astype(F32) + sums_ref[1, g].astype(F32)
        dw_out[:, g * QW:(g + 1) * QW] = got[:, 0:QW]
        dw_out[:, 2048 + g * HD:2048 + (g + 1) * HD] = got[:, QW:QW + HD]
        dw_out[:, 2560 + g * HD:2560 + (g + 1) * HD] = got[:, QW + HD:GW]
    for copy in copies:
        copy.wait()


def body(inputs, w_qkv, random_blocks, d_out):
    dma = pltpu.SemaphoreType.DMA
    vm = pltpu.VMEM
    hbm = pl.BlockSpec(memory_space=pl.ANY)
    attended, sums = pl.pallas_call(
        kernel,
        out_shape=[jax.ShapeDtypeStruct((RING, TOK, QW), BF), jax.ShapeDtypeStruct((2, RING, 16, GW), BF)],
        in_specs=[pl.BlockSpec(memory_space=pltpu.SMEM), hbm, hbm, hbm],
        out_specs=[hbm, pl.BlockSpec(memory_space=pltpu.VMEM)],
        scratch_shapes=[
            vm((RING, TOK, D), BF),
            vm((D, RING * KV), BF),
            vm((RING, D, QW), BF),
            vm((RING, 2, BLOCK, KV), BF),
            vm((3, TOK, QW), BF),
            vm((QBLOCKS, BLOCK, KV), BF),
            vm((RING, TOK, QW), BF),
            vm((RING, TOK, QW), BF),
            vm((RING, TOK, QW), BF),
            vm((RING, TOK, QW), BF),
            vm((QBLOCKS, BLOCK, KV), F32),
            vm((PICKS + 1, BLOCK, KV), F32),
            vm((8 * BLOCK, KV), BF),
            pltpu.SMEM((PICKS,), jnp.int32),
            pltpu.SMEM((PICKS,), jnp.int32),
            pltpu.SMEM((QBLOCKS,), jnp.int32),
            vm((RING * RING, RING, 32, RING * TOK), BF),
            vm((QBLOCKS, BLOCK, KV), BF),
            vm((2, RING, BLOCK, KV), BF),
            vm((2, LOCAL, BLOCK, KV), BF),
            vm((LOCAL, BLOCK, KV), BF),
            vm((4, RING, 128, QW), BF),
            vm((2, 2, 128, QW), BF),
            vm((2, RING, 128, QW), BF),
            vm((3, 128, QW), BF),
            vm((3, 128, QW), BF),
            vm((4, RING, 128, KV), BF),
            vm((3, RING, 128, KV), BF),
            vm((3, 128, KV), BF),
            vm((3, 128, KV), BF),
            vm((RING, 2, 16, GW), BF),
            vm((2, RING, 16, GW), BF),
            dma((4,)), dma((4,)),
            dma((3,)), dma((3,)), dma((16,)), dma((16,)), dma((3,)), dma((3,)), dma((3,)), dma((3,)), dma((6,)), dma((6,)),
            dma((6,)), dma((6,)), dma((3,)), dma((3,)), dma((6,)), dma((6,)), dma((3,)), dma((3,)), dma((3,)), dma((3,)),
            dma((3,)), dma((3,)), dma((8,)), dma((8,)),
        ],
        compiler_params=pltpu.CompilerParams(collective_id=1, has_side_effects=True, vmem_limit_bytes=62 * 2**20),
        cost_estimate=pl.CostEstimate(flops=13 * 10**9, bytes_accessed=20 * 2**20, transcendentals=2**22),
        name="attention_weight_gradient",
    )(random_blocks, inputs[0], w_qkv, d_out[0])
    attended, d_wqkv = pl.pallas_call(
        results_kernel,
        out_shape=[jax.ShapeDtypeStruct((TOK, D), BF), jax.ShapeDtypeStruct((16, RING * GW), F32)],
        in_specs=[hbm, pl.BlockSpec(memory_space=pltpu.VMEM)],
        out_specs=[hbm, pl.BlockSpec(memory_space=pltpu.VMEM)],
        scratch_shapes=[dma((RING,))],
        name="results",
    )(attended, sums)
    return attended[None], d_wqkv


def solution(mesh):
    return jax.shard_map(
        body,
        mesh=mesh,
        in_specs=(P("dp", "seq", None), P(), P(), P("dp", "seq", None)),
        out_specs=(P("dp", "seq", None), P(("seq", "dp"), None)),
        check_vma=False,
    )
```

```python
import jax
import jax.numpy as jnp
from jax import lax
from jax.experimental import pallas as pl
from jax.experimental.pallas import tpu as pltpu
from jax.sharding import PartitionSpec as P

RING = 4
TOK = 256
BLOCK = 128
D = 2048
HD = 128
GROUP = 4
QW = GROUP * HD
KV = 2 * HD
GW = QW + KV
QBLOCKS = 32
NRAND = 3
LOCAL = 2 * RING
PICKS = LOCAL * NRAND
SCALE = HD ** -0.5
EXP2_SCALE = SCALE * 1.4426950408889634
BF = jnp.bfloat16
F32 = jnp.float32
MESH = pl.DeviceIdType.MESH


def places():
    s, d = lax.axis_index("seq"), lax.axis_index("dp")
    x, y, z, c = s // RING, s % RING, d // 2, d % 2
    return x + c * (y - x), y + c * (x - y), z, c


def shard_of(c, q, r):
    return q * (RING - 3 * c) + r * (1 + 3 * c)


def turn(i, steps):
    return lax.rem(i + steps, RING)


def wait_in(ref, sem):
    pltpu.make_async_copy(ref, ref, sem).wait()


def dot(a, b):
    return jnp.dot(a, b, preferred_element_type=F32)


def kernel(rb, x_ref, w_ref, g_ref, att_out, fin_out,
           xown, wkv, wq, gown, kvown, qown, kvall, qall, gall, attb, dqb, near, terms, kcat, last,
           xt, dkvs, dkv_far, dkv_in, dkv, zs, z_far, zin, qs_, qin, ks, kin, kzs, kzin, fs, fin,
           local_sem, wq_sem, g_sem, a_send, a_recv, kv_send, kv_recv, q_send, q_recv, g_send, g_recv, x_send, x_recv,
           dkv_send, dkv_recv, att_send, att_recv, z_send, z_recv, dq_send, dq_recv, k_send, k_recv, kz_send, kz_recv,
           f_send, f_recv):
    q, r, z, c = places()
    rs = [turn(r, k) for k in (1, 3, 2)]
    qs = [turn(q, k) for k in (1, 3, 2)]
    zz = [turn(z, k) for k in (1, 3, 2)]
    up, down, far = rs
    r_from = (down, up, far)
    q_from = (qs[1], qs[0], qs[2])

    def peer(q_, r_, z_):
        return (shard_of(c, q_, r_), z_ * 2 + c)

    load_x = pltpu.make_async_copy(x_ref, xown, local_sem.at[0])
    load_x.start()
    load_wkv = pltpu.make_async_copy(w_ref.at[:, pl.ds(RING * QW, RING * KV)], wkv, local_sem.at[1])
    load_wkv.start()
    load_g = [pltpu.make_async_copy(g_ref.at[:, pl.ds(pl.multiple_of(to * QW, QW), QW)], dst, g_sem.at[k])
              for k, (to, dst) in enumerate(((up, gown.at[0]), (down, gown.at[1]), (far, gown.at[2]), (r, gall.at[r])))]
    load_wq = [pltpu.make_async_copy(w_ref.at[:, pl.ds(pl.multiple_of(to * QW, QW), QW)], wq.at[k], wq_sem.at[k])
               for k, to in enumerate((up, down, far, r))]

    barrier = pltpu.get_barrier_semaphore()
    met = [peer(q, rs[k], z) for k in range(3)] + [peer(qs[k], r, z) for k in range(3)]
    met += [peer(q, r, zz[k]) for k in range(3)]
    met += [(shard_of(c, q, turn(r, k)), z * 2 + 1 - c) for k in range(RING)]
    met += [(shard_of(c, turn(q, k), r), z * 2 + 1 - c) for k in range(RING)]
    for device in met:
        pl.semaphore_signal(barrier, inc=1, device_id=device, device_id_type=MESH)

    sent = []

    def remote(src, dst, send, recv, to):
        copy = pltpu.make_async_remote_copy(src_ref=src, dst_ref=dst, send_sem=send, recv_sem=recv,
                                            device_id=to, device_id_type=MESH)
        sent.append(copy)
        return copy

    def step_j(step):
        return turn(r, jnp.where(step == 0, 0, jnp.where(step == 1, 3, step - 1)))

    def place_of(n):
        s = n // 2
        return (s + c * ((s % RING) * RING + s // RING - s)) * 2 + n % 2

    load_x.wait()
    load_wkv.wait()
    for copy in load_wq:
        copy.start()
    for copy in load_g:
        copy.start()
    x_own = xown[...]
    for part in range(4):
        got = dot(x_own, wkv[:, part * 256:(part + 1) * 256]).astype(BF)
        cols = slice(0, HD) if part < 2 else slice(HD, KV)
        for n in range(2):
            kvown[part % 2 * 2 + n, :, :, cols] = got[:, n * HD:(n + 1) * HD].reshape(2, BLOCK, HD)

    pl.semaphore_wait(barrier, len(met))

    def slot(j):
        return kvall.at[pl.ds((q * RING + j) * 2, 2)]

    for k in range(3):
        remote(kvown.at[rs[k]], slot(r), a_send.at[k], a_recv.at[k], peer(q, rs[k], z)).start()

    def pass_on(step, src, j):
        for k in range(2):
            remote(src, slot(j), kv_send.at[step * 4 + k], kv_recv.at[step * 4 + k], peer(qs[k], r, z)).start()

    def pass_on_block(step, j):
        for k in range(2):
            whole = kvall.at[pl.ds((q_from[k] * RING + j) * 2, 2)]
            wait_in(whole, kv_recv.at[step * 4 + k])
            block = kvall.at[pl.ds((q_from[k] * RING + j) * 2 + k, 1)]
            remote(block, block, kv_send.at[step * 4 + 2 + k], kv_recv.at[step * 4 + 2 + k], peer(qs[k], r, z)).start()

    def project_queries(k):
        load_wq[k].wait()
        for part in range(2):
            cols = slice(part * 256, (part + 1) * 256)
            got = dot(x_own, wq[k, :, cols]).astype(BF)
            if k < 3:
                qown[k, :, cols] = got
            else:
                qall[r, :, cols] = got

    q_copies = [remote(qown.at[k], qall.at[r], q_send.at[k], q_recv.at[k], peer(q, rs[k], z)) for k in range(3)]
    g_copies = [remote(gown.at[k], gall.at[r], g_send.at[k], g_recv.at[k], peer(q, rs[k], z)) for k in range(3)]
    halves = (pl.ds(0, 2 * RING), pl.ds(2 * RING, 2 * RING))
    x_copies = [remote(xt.at[r, halves[half]], xt.at[r, halves[half]], x_send.at[n], x_recv.at[n], peer(q, to, z))
                for n, (half, to) in enumerate(((0, up), (1, down), (1, up), (0, down)))]
    x_on = [remote(xt.at[down, halves[0]], xt.at[down, halves[0]], x_send.at[4], x_recv.at[4], peer(q, up, z)),
            remote(xt.at[up, halves[1]], xt.at[up, halves[1]], x_send.at[5], x_recv.at[5], peer(q, down, z))]

    pass_on(0, kvown.at[r], r)
    kvall[pl.ds((q * RING + r) * 2, 2)] = kvown[r]
    for copy in load_g:
        copy.wait()
    for k in range(2):
        g_copies[k].start()
    xt[r] = x_own.T.reshape(RING * RING, RING, 32, TOK)
    near[...] = jnp.zeros_like(near)
    terms[PICKS] = jnp.zeros((BLOCK, KV), F32)
    for n in range(QBLOCKS):
        last[n] = PICKS
    for k in range(2):
        wait_in(slot(r_from[k]), a_recv.at[k])
        pass_on(k + 1, slot(r_from[k]), r_from[k])
    project_queries(0)
    wait_in(slot(far), a_recv.at[2])
    pass_on(3, slot(far), far)
    pass_on_block(0, r)
    project_queries(1)
    pass_on_block(1, down)
    pass_on_block(2, up)
    project_queries(2)
    pass_on_block(3, far)
    project_queries(3)

    for step, j in enumerate((r, down, up, far)):
        for k in range(2):
            wait_in(kvall.at[pl.ds((qs[2] * RING + j) * 2 + k, 1)], kv_recv.at[step * 4 + 2 + k])
    for k in range(2):
        q_copies[k].start()

    def attend(i, _):
        @pl.when(i == 1)
        def _():
            x_copies[0].start()
            x_copies[1].start()

        @pl.when(i == 2)
        def _():
            q_copies[2].start()
            g_copies[2].start()

        for k in range(3):
            @pl.when(i == 2 * k + 2)
            def _():
                wait_in(qall.at[r_from[k]], q_recv.at[k])
                wait_in(gall.at[r_from[k]], g_recv.at[k])

        @pl.when(i == 3)
        def _():
            x_copies[2].start()
            x_copies[3].start()

        @pl.when(i == 6)
        def _():
            wait_in(xt.at[down, halves[0]], x_recv.at[0])
            x_on[0].start()
            wait_in(xt.at[up, halves[1]], x_recv.at[1])
            x_on[1].start()

        j = step_j(i // 2)
        b = shard_of(c, q, j) * 2 + i % 2
        rows = pl.ds(pl.multiple_of((i % 2) * BLOCK, BLOCK), BLOCK)
        near_ids = [place_of(n) for n in (lax.rem(b + QBLOCKS - 1, QBLOCKS), b, lax.rem(b + 1, QBLOCKS),
                                          jnp.int32(0), jnp.int32(1))]
        far_ids = [place_of(rb[b, n]) for n in range(NRAND)]
        listed = near_ids + far_ids
        for l, n in enumerate(listed):
            kcat[pl.ds(l * BLOCK, BLOCK), :] = kvall[n]
        keys, values = kcat[:, :HD], kcat[:, HD:]
        heads = [slice(h * HD, (h + 1) * HD) for h in range(GROUP)]
        queries = jnp.concatenate([qall[j, rows, h] for h in heads], axis=0)
        grads = jnp.concatenate([gall[j, rows, h] for h in heads], axis=0)
        nt = (((1,), (1,)), ((), ()))
        scores = lax.dot_general(keys, queries, nt, preferred_element_type=F32)
        peak = jnp.max(scores, axis=0, keepdims=True)
        expos = jnp.exp2((scores - peak) * EXP2_SCALE)
        probs = expos * (1.0 / jnp.sum(expos, axis=0, keepdims=True))
        weights = probs.astype(BF)
        dprob = lax.dot_general(values, grads, nt, preferred_element_type=F32)
        attended = dot(values.T, weights)
        mean = jnp.sum(probs * dprob, axis=0, keepdims=True)
        dweights = (probs * (dprob - mean)).astype(BF)
        d_query = dot(keys.T, dweights) * SCALE
        for h in heads:
            attb[j, rows, h] = attended[:, h].T.astype(BF)
            dqb[j, rows, h] = d_query[:, h].T.astype(BF)
        d_key = dot(dweights, queries) * SCALE
        d_value = dot(weights, grads)
        for l, n in enumerate(near_ids):
            at = slice(l * BLOCK, (l + 1) * BLOCK)
            near[n, :, 0:HD] += d_key[at]
            near[n, :, HD:] += d_value[at]
        for l in range(NRAND):
            at = slice((5 + l) * BLOCK, (6 + l) * BLOCK)
            before = terms[last[far_ids[l]]]
            terms[i * NRAND + l, :, 0:HD] = before[:, 0:HD] + d_key[at]
            terms[i * NRAND + l, :, HD:] = before[:, HD:] + d_value[at]
        for n in range(QBLOCKS):
            got = last[n]
            for l in range(NRAND):
                got = jnp.where(far_ids[l] == n, i * NRAND + l, got)
            last[n] = got
        return 0

    lax.fori_loop(0, LOCAL, attend, 0)

    def ring_far(chunk, landed, send, recv, to):
        for k in range(2):
            remote(chunk(2, k), landed.at[k], send.at[k], recv.at[k], to[k]).start()

    def ring_free(chunk, arrived, send, recv, to):
        for k in range(2):
            remote(chunk(k, 1 - k), arrived(k, 1 - k), send.at[2 + k], recv.at[2 + k], to[k]).start()

    def ring_rest(chunk, landed, arrived, send, recv, to):
        for k in range(2):
            wait_in(landed.at[k], recv.at[k])
            chunk(k, k)[...] = (chunk(k, k)[...].astype(F32) + landed[k].astype(F32)).astype(BF)
            remote(chunk(k, k), arrived(k, k), send.at[4 + k], recv.at[4 + k], to[k]).start()

    def ring_wait(arrived, recv):
        for k in range(2):
            wait_in(arrived(k, 1 - k), recv.at[2 + k])
            wait_in(arrived(k, k), recv.at[4 + k])

    def dkv_chunk(k, half):
        return dkvs.at[pl.ds(qs[k] * LOCAL + half * RING, RING)]

    def dkv_arrived(k, half):
        return dkv_in.at[k, pl.ds(half * RING, RING)]

    q_peers = [peer(qs[k], r, z) for k in range(2)]
    z_peers = [peer(q, r, zz[k]) for k in range(2)]

    def gather_terms(k):
        def one(n, _):
            at = qs[k] * LOCAL + n
            dkvs[at] = (near[at] + terms[last[at]]).astype(BF)
            return 0

        lax.fori_loop(0, LOCAL, one, 0)

    gather_terms(2)
    gather_terms(0)
    gather_terms(1)
    wait_in(xt.at[down, halves[1]], x_recv.at[2])
    wait_in(xt.at[up, halves[0]], x_recv.at[3])
    wait_in(xt.at[far, halves[0]], x_recv.at[4])
    wait_in(xt.at[far, halves[1]], x_recv.at[5])
    dq_all = dqb[...].reshape(RING * TOK, QW)

    def rows_of(z_, q_):
        return jnp.concatenate([jnp.concatenate([xt[j, shard_of(c, q_, n), z_] for n in range(RING)], axis=0)
                                for j in range(RING)], axis=1)

    def z_chunk(k, half):
        return zs.at[k, pl.ds(half * 2, 2)]

    def z_arrived(k, half):
        return zin.at[k, pl.ds(half * 2, 2)]

    def z_product(k, z_):
        rows = jnp.concatenate([rows_of(z_, q_) for q_ in range(RING)], axis=0)
        zs[k] = dot(rows, dq_all).astype(BF).reshape(RING, 128, QW)

    z_product(2, zz[2])
    ring_far(z_chunk, z_far, z_send, z_recv, z_peers)
    ring_far(dkv_chunk, dkv_far, dkv_send, dkv_recv, q_peers)
    ring_free(dkv_chunk, dkv_arrived, dkv_send, dkv_recv, q_peers)
    z_product(0, zz[0])
    z_product(1, zz[1])
    ring_free(z_chunk, z_arrived, z_send, z_recv, z_peers)
    ring_rest(dkv_chunk, dkv_far, dkv_arrived, dkv_send, dkv_recv, q_peers)
    z_product(3, z)

    ring_wait(dkv_arrived, dkv_recv)

    def add_terms(n, _):
        at = q * LOCAL + n
        got = near[at] + terms[last[at]]
        for k in range(2):
            got += dkv_in[k, n].astype(F32)
        dkv[n] = got.astype(BF)
        return 0

    lax.fori_loop(0, LOCAL, add_terms, 0)
    dkv_all = dkv[...].reshape(RING * TOK, KV)

    def k_product(k, q_):
        rows = jnp.concatenate([rows_of(z_, q_) for z_ in range(RING)], axis=0)
        ks[k] = dot(rows, dkv_all).astype(BF).reshape(RING, 128, KV)

    for k in (2, 0, 1):
        k_product(k, qs[k])
        remote(ks.at[k], kin.at[k], k_send.at[k], k_recv.at[k], peer(qs[k], r, z)).start()
    k_product(3, q)
    ring_rest(z_chunk, z_far, z_arrived, z_send, z_recv, z_peers)
    for k in range(3):
        wait_in(kin.at[k], k_recv.at[k])
    for k in range(3):
        got = ks[3, zz[k]].astype(F32)
        for n in range(3):
            got += kin[n, zz[k]].astype(F32)
        kzs[k] = got.astype(BF)
        remote(kzs.at[k], kzin.at[k], kz_send.at[k], kz_recv.at[k], peer(q, r, zz[k])).start()

    for k in range(3):
        remote(attb.at[rs[k]], att_out.at[r],
               att_send.at[k], att_recv.at[k], peer(q, rs[k], z)).start()
    own_att = pltpu.make_async_copy(attb.at[r], att_out.at[r], local_sem.at[3])
    own_att.start()
    ring_wait(z_arrived, z_recv)
    for k in range(3):
        got = zs[3, qs[k]].astype(F32)
        for n in range(2):
            got += zin[n, qs[k]].astype(F32)
        qs_[k] = got.astype(BF)
        remote(qs_.at[k], qin.at[k], dq_send.at[k], dq_recv.at[k], peer(qs[k], r, z)).start()
    own_q = zs[3, q].astype(F32)
    own_k = ks[3, z].astype(F32)
    for n in range(3):
        own_k += kin[n, z].astype(F32)
    for n in range(2):
        own_q += zin[n, q].astype(F32)
    for k in range(3):
        wait_in(qin.at[k], dq_recv.at[k])
        wait_in(kzin.at[k], kz_recv.at[k])
    for k in range(3):
        own_q += qin[k].astype(F32)
        own_k += kzin[k].astype(F32)
    fs[:, :, :, 0:QW] = own_q.astype(BF).reshape(RING, 2, 16, QW)
    fs[:, :, :, QW:GW] = own_k.astype(BF).reshape(RING, 2, 16, KV)

    for k in range(RING):
        to = turn(r, k)
        if k:
            remote(fs.at[to, c], fin.at[0, k], f_send.at[k], f_recv.at[k], (shard_of(c, q, to), z * 2 + c)).start()
        remote(fs.at[to, 1 - c], fin.at[1, k], f_send.at[RING + k], f_recv.at[RING + k],
               (shard_of(c, q, to), z * 2 + 1 - c)).start()
    fin[0, 0] = fs[r, c]
    for k in range(RING):
        if k:
            wait_in(fin.at[0, k], f_recv.at[k])
        wait_in(fin.at[1, k], f_recv.at[RING + k])
    for g in range(RING):
        fin_out[0, g] = fin[0, lax.rem(r + RING - g, RING)]
        fin_out[1, g] = fin[1, lax.rem(q + RING - g, RING)]

    for k in range(3):
        wait_in(att_out.at[r_from[k]], att_recv.at[k])
    for copy in sent:
        copy.wait_send()
    own_att.wait()


def results_kernel(att_ref, sums_ref, att_out, dw_out):
    for g in range(RING):
        att_out[:, g * QW:(g + 1) * QW] = att_ref[g]
        got = sums_ref[0, g].astype(F32) + sums_ref[1, g].astype(F32)
        dw_out[:, g * QW:(g + 1) * QW] = got[:, 0:QW]
        dw_out[:, 2048 + g * HD:2048 + (g + 1) * HD] = got[:, QW:QW + HD]
        dw_out[:, 2560 + g * HD:2560 + (g + 1) * HD] = got[:, QW + HD:GW]


def body(inputs, w_qkv, random_blocks, d_out):
    dma = pltpu.SemaphoreType.DMA
    vm = pltpu.VMEM
    hbm = pl.BlockSpec(memory_space=pl.ANY)
    attended, sums = pl.pallas_call(
        kernel,
        out_shape=[jax.ShapeDtypeStruct((RING, TOK, QW), BF), jax.ShapeDtypeStruct((2, RING, 16, GW), BF)],
        in_specs=[pl.BlockSpec(memory_space=pltpu.SMEM), hbm, hbm, hbm],
        out_specs=[hbm, pl.BlockSpec(memory_space=pltpu.VMEM)],
        scratch_shapes=[
            vm((TOK, D), BF),
            vm((D, RING * KV), BF),
            vm((RING, D, QW), BF),
            vm((3, TOK, QW), BF),
            vm((RING, 2, BLOCK, KV), BF),
            vm((3, TOK, QW), BF),
            vm((QBLOCKS, BLOCK, KV), BF),
            vm((RING, TOK, QW), BF),
            vm((RING, TOK, QW), BF),
            vm((RING, TOK, QW), BF),
            vm((RING, TOK, QW), BF),
            vm((QBLOCKS, BLOCK, KV), F32),
            vm((PICKS + 1, BLOCK, KV), F32),
            vm((8 * BLOCK, KV), BF),
            pltpu.SMEM((QBLOCKS,), jnp.int32),
            vm((RING, RING * RING, RING, 32, TOK), BF),
            vm((QBLOCKS, BLOCK, KV), BF),
            vm((2, RING, BLOCK, KV), BF),
            vm((2, LOCAL, BLOCK, KV), BF),
            vm((LOCAL, BLOCK, KV), BF),
            vm((4, RING, 128, QW), BF),
            vm((2, 2, 128, QW), BF),
            vm((2, RING, 128, QW), BF),
            vm((3, 128, QW), BF),
            vm((3, 128, QW), BF),
            vm((4, RING, 128, KV), BF),
            vm((3, RING, 128, KV), BF),
            vm((3, 128, KV), BF),
            vm((3, 128, KV), BF),
            vm((RING, 2, 16, GW), BF),
            vm((2, RING, 16, GW), BF),
            dma((4,)), dma((4,)), dma((4,)),
            dma((3,)), dma((3,)), dma((16,)), dma((16,)), dma((3,)), dma((3,)), dma((3,)), dma((3,)), dma((6,)), dma((6,)),
            dma((6,)), dma((6,)), dma((3,)), dma((3,)), dma((6,)), dma((6,)), dma((3,)), dma((3,)), dma((3,)), dma((3,)),
            dma((3,)), dma((3,)), dma((8,)), dma((8,)),
        ],
        compiler_params=pltpu.CompilerParams(collective_id=1, has_side_effects=True, vmem_limit_bytes=62 * 2**20),
        cost_estimate=pl.CostEstimate(flops=13 * 10**9, bytes_accessed=20 * 2**20, transcendentals=2**22),
        name="attention_weight_gradient",
    )(random_blocks, inputs[0], w_qkv, d_out[0])
    attended, d_wqkv = pl.pallas_call(
        results_kernel,
        out_shape=[jax.ShapeDtypeStruct((TOK, D), BF), jax.ShapeDtypeStruct((16, RING * GW), F32)],
        in_specs=[pl.BlockSpec(memory_space=pltpu.VMEM)] * 2,
        out_specs=[pl.BlockSpec(memory_space=pltpu.VMEM)] * 2,
        name="results",
    )(attended, sums)
    return attended[None], d_wqkv


def solution(mesh):
    return jax.shard_map(
        body,
        mesh=mesh,
        in_specs=(P("dp", "seq", None), P(), P(), P("dp", "seq", None)),
        out_specs=(P("dp", "seq", None), P(("seq", "dp"), None)),
        check_vma=False,
    )
```

```python
import jax
import jax.numpy as jnp
from jax import lax
from jax.experimental import pallas as pl
from jax.experimental.pallas import tpu as pltpu
from jax.sharding import PartitionSpec as P

RING = 4
TOK = 256
BLOCK = 128
D = 2048
HD = 128
GROUP = 4
QW = GROUP * HD
KV = 2 * HD
GW = QW + KV
QBLOCKS = 32
NRAND = 3
LOCAL = 2 * RING
PICKS = LOCAL * NRAND
SCALE = HD ** -0.5
EXP2_SCALE = SCALE * 1.4426950408889634
BF = jnp.bfloat16
F32 = jnp.float32
MESH = pl.DeviceIdType.MESH


def places():
    s, d = lax.axis_index("seq"), lax.axis_index("dp")
    x, y, z, c = s // RING, s % RING, d // 2, d % 2
    return x + c * (y - x), y + c * (x - y), z, c


def shard_of(c, q, r):
    return q * (RING - 3 * c) + r * (1 + 3 * c)


def turn(i, steps):
    return lax.rem(i + steps, RING)


def wait_in(ref, sem):
    pltpu.make_async_copy(ref, ref, sem).wait()


def dot(a, b):
    return jnp.dot(a, b, preferred_element_type=F32)


def kernel(rb_ref, x_ref, w_ref, g_ref, att_out, fin_out,
           rb, rb_sem, xown, wkv, wq, gown, kvown, qown, kvall, qall, gall, attb, dqb, near, terms, kcat, last,
           xt, dkvs, dkv_far, dkv_in, dkv, zs, z_far, zin, qs_, qin, ks, kin, kzs, kzin, fs, fin,
           local_sem, wq_sem, g_sem, a_send, a_recv, kv_send, kv_recv, q_send, q_recv, g_send, g_recv, x_send, x_recv,
           dkv_send, dkv_recv, att_send, att_recv, z_send, z_recv, dq_send, dq_recv, k_send, k_recv, kz_send, kz_recv,
           f_send, f_recv):
    q, r, z, c = places()
    rs = [turn(r, k) for k in (1, 3, 2)]
    qs = [turn(q, k) for k in (1, 3, 2)]
    zz = [turn(z, k) for k in (1, 3, 2)]
    up, down, far = rs
    r_from = (down, up, far)
    q_from = (qs[1], qs[0], qs[2])

    def peer(q_, r_, z_):
        return (shard_of(c, q_, r_), z_ * 2 + c)

    load_x = pltpu.make_async_copy(x_ref, xown, local_sem.at[0])
    load_rb = pltpu.make_async_copy(rb_ref, rb, rb_sem)
    load_rb.start()
    load_x.start()
    load_wkv = pltpu.make_async_copy(w_ref.at[:, pl.ds(RING * QW, RING * KV)], wkv, local_sem.at[1])
    load_wkv.start()
    load_g = [pltpu.make_async_copy(g_ref.at[:, pl.ds(pl.multiple_of(to * QW, QW), QW)], dst, g_sem.at[k])
              for k, (to, dst) in enumerate(((up, gown.at[0]), (down, gown.at[1]), (far, gown.at[2]), (r, gall.at[r])))]
    load_wq = [pltpu.make_async_copy(w_ref.at[:, pl.ds(pl.multiple_of(to * QW, QW), QW)], wq.at[k], wq_sem.at[k])
               for k, to in enumerate((up, down, far, r))]

    barrier = pltpu.get_barrier_semaphore()
    met = [peer(q, rs[k], z) for k in range(3)] + [peer(qs[k], r, z) for k in range(3)]
    met += [peer(q, r, zz[k]) for k in range(3)]
    met += [(shard_of(c, q, turn(r, k)), z * 2 + 1 - c) for k in range(RING)]
    met += [(shard_of(c, turn(q, k), r), z * 2 + 1 - c) for k in range(RING)]
    for device in met:
        pl.semaphore_signal(barrier, inc=1, device_id=device, device_id_type=MESH)

    sent = []

    def remote(src, dst, send, recv, to):
        copy = pltpu.make_async_remote_copy(src_ref=src, dst_ref=dst, send_sem=send, recv_sem=recv,
                                            device_id=to, device_id_type=MESH)
        sent.append(copy)
        return copy

    def step_j(step):
        return turn(r, jnp.where(step == 0, 0, jnp.where(step == 1, 3, step - 1)))

    def place_of(n):
        s = n // 2
        return (s + c * ((s % RING) * RING + s // RING - s)) * 2 + n % 2

    load_rb.wait()
    load_x.wait()
    load_wkv.wait()
    for copy in load_wq:
        copy.start()
    for copy in load_g:
        copy.start()
    x_own = xown[...]
    for part in range(4):
        got = dot(x_own, wkv[:, part * 256:(part + 1) * 256]).astype(BF)
        cols = slice(0, HD) if part < 2 else slice(HD, KV)
        for n in range(2):
            kvown[part % 2 * 2 + n, :, :, cols] = got[:, n * HD:(n + 1) * HD].reshape(2, BLOCK, HD)

    pl.semaphore_wait(barrier, len(met))

    def slot(j):
        return kvall.at[pl.ds((q * RING + j) * 2, 2)]

    for k in range(3):
        remote(kvown.at[rs[k]], slot(r), a_send.at[k], a_recv.at[k], peer(q, rs[k], z)).start()

    def pass_on(step, src, j):
        for k in range(2):
            remote(src, slot(j), kv_send.at[step * 4 + k], kv_recv.at[step * 4 + k], peer(qs[k], r, z)).start()

    def pass_on_block(step, j):
        for k in range(2):
            whole = kvall.at[pl.ds((q_from[k] * RING + j) * 2, 2)]
            wait_in(whole, kv_recv.at[step * 4 + k])
            block = kvall.at[pl.ds((q_from[k] * RING + j) * 2 + k, 1)]
            remote(block, block, kv_send.at[step * 4 + 2 + k], kv_recv.at[step * 4 + 2 + k], peer(qs[k], r, z)).start()

    def project_queries(k):
        load_wq[k].wait()
        for part in range(2):
            cols = slice(part * 256, (part + 1) * 256)
            got = dot(x_own, wq[k, :, cols]).astype(BF)
            if k < 3:
                qown[k, :, cols] = got
            else:
                qall[r, :, cols] = got

    q_copies = [remote(qown.at[k], qall.at[r], q_send.at[k], q_recv.at[k], peer(q, rs[k], z)) for k in range(3)]
    g_copies = [remote(gown.at[k], gall.at[r], g_send.at[k], g_recv.at[k], peer(q, rs[k], z)) for k in range(3)]
    halves = (pl.ds(0, 2 * RING), pl.ds(2 * RING, 2 * RING))
    x_copies = [remote(xt.at[r, halves[half]], xt.at[r, halves[half]], x_send.at[n], x_recv.at[n], peer(q, to, z))
                for n, (half, to) in enumerate(((0, up), (1, down), (1, up), (0, down)))]
    x_on = [remote(xt.at[down, halves[0]], xt.at[down, halves[0]], x_send.at[4], x_recv.at[4], peer(q, up, z)),
            remote(xt.at[up, halves[1]], xt.at[up, halves[1]], x_send.at[5], x_recv.at[5], peer(q, down, z))]

    pass_on(0, kvown.at[r], r)
    kvall[pl.ds((q * RING + r) * 2, 2)] = kvown[r]
    for copy in load_g:
        copy.wait()
    for k in range(2):
        g_copies[k].start()
    xt[r] = x_own.T.reshape(RING * RING, RING, 32, TOK)
    near[...] = jnp.zeros_like(near)
    terms[PICKS] = jnp.zeros((BLOCK, KV), F32)
    for n in range(QBLOCKS):
        last[n] = PICKS
    for k in range(2):
        wait_in(slot(r_from[k]), a_recv.at[k])
        pass_on(k + 1, slot(r_from[k]), r_from[k])
    project_queries(0)
    wait_in(slot(far), a_recv.at[2])
    pass_on(3, slot(far), far)
    pass_on_block(0, r)
    project_queries(1)
    pass_on_block(1, down)
    pass_on_block(2, up)
    project_queries(2)
    pass_on_block(3, far)
    project_queries(3)

    for step, j in enumerate((r, down, up, far)):
        for k in range(2):
            wait_in(kvall.at[pl.ds((qs[2] * RING + j) * 2 + k, 1)], kv_recv.at[step * 4 + 2 + k])
    x_copies[0].start()
    x_copies[1].start()
    for k in range(2):
        q_copies[k].start()

    def attend(i, _):
        @pl.when(i == 2)
        def _():
            q_copies[2].start()
            g_copies[2].start()

        for k in range(3):
            @pl.when(i == 2 * k + 2)
            def _():
                wait_in(qall.at[r_from[k]], q_recv.at[k])
                wait_in(gall.at[r_from[k]], g_recv.at[k])

        @pl.when(i == 1)
        def _():
            x_copies[2].start()
            x_copies[3].start()

        @pl.when(i == 5)
        def _():
            wait_in(xt.at[down, halves[0]], x_recv.at[0])
            x_on[0].start()
            wait_in(xt.at[up, halves[1]], x_recv.at[1])
            x_on[1].start()

        j = step_j(i // 2)
        b = shard_of(c, q, j) * 2 + i % 2
        rows = pl.ds(pl.multiple_of((i % 2) * BLOCK, BLOCK), BLOCK)
        near_ids = [place_of(n) for n in (lax.rem(b + QBLOCKS - 1, QBLOCKS), b, lax.rem(b + 1, QBLOCKS),
                                          jnp.int32(0), jnp.int32(1))]
        far_ids = [place_of(rb[n, b]) for n in range(NRAND)]
        listed = near_ids + far_ids
        for l, n in enumerate(listed):
            kcat[pl.ds(l * BLOCK, BLOCK), :] = kvall[n]
        keys, values = kcat[:, :HD], kcat[:, HD:]
        heads = [slice(h * HD, (h + 1) * HD) for h in range(GROUP)]
        queries = jnp.concatenate([qall[j, rows, h] for h in heads], axis=0)
        grads = jnp.concatenate([gall[j, rows, h] for h in heads], axis=0)
        nt = (((1,), (1,)), ((), ()))
        scores = lax.dot_general(keys, queries, nt, preferred_element_type=F32)
        peak = jnp.max(scores, axis=0, keepdims=True)
        expos = jnp.exp2((scores - peak) * EXP2_SCALE)
        probs = expos * (1.0 / jnp.sum(expos, axis=0, keepdims=True))
        weights = probs.astype(BF)
        dprob = lax.dot_general(values, grads, nt, preferred_element_type=F32)
        attended = dot(values.T, weights)
        mean = jnp.sum(probs * dprob, axis=0, keepdims=True)
        dweights = (probs * (dprob - mean)).astype(BF)
        d_query = dot(keys.T, dweights) * SCALE
        for h in heads:
            attb[j, rows, h] = attended[:, h].T.astype(BF)
            dqb[j, rows, h] = d_query[:, h].T.astype(BF)
        d_key = dot(dweights, queries) * SCALE
        d_value = dot(weights, grads)
        for l, n in enumerate(near_ids):
            at = slice(l * BLOCK, (l + 1) * BLOCK)
            near[n, :, 0:HD] += d_key[at]
            near[n, :, HD:] += d_value[at]
        for l in range(NRAND):
            at = slice((5 + l) * BLOCK, (6 + l) * BLOCK)
            before = terms[last[far_ids[l]]]
            terms[i * NRAND + l, :, 0:HD] = before[:, 0:HD] + d_key[at]
            terms[i * NRAND + l, :, HD:] = before[:, HD:] + d_value[at]
        for n in range(QBLOCKS):
            got = last[n]
            for l in range(NRAND):
                got = jnp.where(far_ids[l] == n, i * NRAND + l, got)
            last[n] = got
        return 0

    lax.fori_loop(0, LOCAL, attend, 0)

    def ring_far(chunk, landed, send, recv, to):
        for k in range(2):
            remote(chunk(2, k), landed.at[k], send.at[k], recv.at[k], to[k]).start()

    def ring_free(chunk, arrived, send, recv, to):
        for k in range(2):
            remote(chunk(k, 1 - k), arrived(k, 1 - k), send.at[2 + k], recv.at[2 + k], to[k]).start()

    def ring_rest(chunk, landed, arrived, send, recv, to):
        for k in range(2):
            wait_in(landed.at[k], recv.at[k])
            chunk(k, k)[...] = (chunk(k, k)[...].astype(F32) + landed[k].astype(F32)).astype(BF)
            remote(chunk(k, k), arrived(k, k), send.at[4 + k], recv.at[4 + k], to[k]).start()

    def ring_wait(arrived, recv):
        for k in range(2):
            wait_in(arrived(k, 1 - k), recv.at[2 + k])
            wait_in(arrived(k, k), recv.at[4 + k])

    def dkv_chunk(k, half):
        return dkvs.at[pl.ds(qs[k] * LOCAL + half * RING, RING)]

    def dkv_arrived(k, half):
        return dkv_in.at[k, pl.ds(half * RING, RING)]

    q_peers = [peer(qs[k], r, z) for k in range(2)]
    z_peers = [peer(q, r, zz[k]) for k in range(2)]

    def gather_terms(k):
        def one(n, _):
            at = qs[k] * LOCAL + n
            dkvs[at] = (near[at] + terms[last[at]]).astype(BF)
            return 0

        lax.fori_loop(0, LOCAL, one, 0)

    gather_terms(2)
    gather_terms(0)
    gather_terms(1)
    wait_in(xt.at[down, halves[1]], x_recv.at[2])
    wait_in(xt.at[up, halves[0]], x_recv.at[3])
    wait_in(xt.at[far, halves[0]], x_recv.at[4])
    wait_in(xt.at[far, halves[1]], x_recv.at[5])
    dq_all = dqb[...].reshape(RING * TOK, QW)

    def rows_of(z_, q_):
        return jnp.concatenate([jnp.concatenate([xt[j, shard_of(c, q_, n), z_] for n in range(RING)], axis=0)
                                for j in range(RING)], axis=1)

    def z_chunk(k, half):
        return zs.at[k, pl.ds(half * 2, 2)]

    def z_arrived(k, half):
        return zin.at[k, pl.ds(half * 2, 2)]

    def z_product(k, z_):
        rows = jnp.concatenate([rows_of(z_, q_) for q_ in range(RING)], axis=0)
        zs[k] = dot(rows, dq_all).astype(BF).reshape(RING, 128, QW)

    z_product(2, zz[2])
    ring_far(z_chunk, z_far, z_send, z_recv, z_peers)
    ring_far(dkv_chunk, dkv_far, dkv_send, dkv_recv, q_peers)
    ring_free(dkv_chunk, dkv_arrived, dkv_send, dkv_recv, q_peers)
    z_product(0, zz[0])
    z_product(1, zz[1])
    ring_free(z_chunk, z_arrived, z_send, z_recv, z_peers)
    ring_rest(dkv_chunk, dkv_far, dkv_arrived, dkv_send, dkv_recv, q_peers)
    z_product(3, z)

    ring_wait(dkv_arrived, dkv_recv)

    def add_terms(n, _):
        at = q * LOCAL + n
        got = near[at] + terms[last[at]]
        for k in range(2):
            got += dkv_in[k, n].astype(F32)
        dkv[n] = got.astype(BF)
        return 0

    lax.fori_loop(0, LOCAL, add_terms, 0)
    dkv_all = dkv[...].reshape(RING * TOK, KV)

    def k_product(k, q_):
        rows = jnp.concatenate([rows_of(z_, q_) for z_ in range(RING)], axis=0)
        ks[k] = dot(rows, dkv_all).astype(BF).reshape(RING, 128, KV)

    for k in (2, 0, 1):
        k_product(k, qs[k])
        remote(ks.at[k], kin.at[k], k_send.at[k], k_recv.at[k], peer(qs[k], r, z)).start()
    k_product(3, q)
    ring_rest(z_chunk, z_far, z_arrived, z_send, z_recv, z_peers)
    for k in range(3):
        wait_in(kin.at[k], k_recv.at[k])
    for k in range(3):
        got = ks[3, zz[k]].astype(F32)
        for n in range(3):
            got += kin[n, zz[k]].astype(F32)
        kzs[k] = got.astype(BF)
        remote(kzs.at[k], kzin.at[k], kz_send.at[k], kz_recv.at[k], peer(q, r, zz[k])).start()

    for k in range(3):
        remote(attb.at[rs[k]], att_out.at[r],
               att_send.at[k], att_recv.at[k], peer(q, rs[k], z)).start()
    own_att = pltpu.make_async_copy(attb.at[r], att_out.at[r], local_sem.at[3])
    own_att.start()
    ring_wait(z_arrived, z_recv)
    for k in range(3):
        got = zs[3, qs[k]].astype(F32)
        for n in range(2):
            got += zin[n, qs[k]].astype(F32)
        qs_[k] = got.astype(BF)
        remote(qs_.at[k], qin.at[k], dq_send.at[k], dq_recv.at[k], peer(qs[k], r, z)).start()
    own_q = zs[3, q].astype(F32)
    own_k = ks[3, z].astype(F32)
    for n in range(3):
        own_k += kin[n, z].astype(F32)
    for n in range(2):
        own_q += zin[n, q].astype(F32)
    for k in range(3):
        wait_in(qin.at[k], dq_recv.at[k])
        wait_in(kzin.at[k], kz_recv.at[k])
    for k in range(3):
        own_q += qin[k].astype(F32)
        own_k += kzin[k].astype(F32)
    fs[:, :, :, 0:QW] = own_q.astype(BF).reshape(RING, 2, 16, QW)
    fs[:, :, :, QW:GW] = own_k.astype(BF).reshape(RING, 2, 16, KV)

    for k in range(RING):
        to = turn(r, k)
        if k:
            remote(fs.at[to, c], fin.at[0, k], f_send.at[k], f_recv.at[k], (shard_of(c, q, to), z * 2 + c)).start()
        remote(fs.at[to, 1 - c], fin.at[1, k], f_send.at[RING + k], f_recv.at[RING + k],
               (shard_of(c, q, to), z * 2 + 1 - c)).start()
    fin[0, 0] = fs[r, c]
    for k in range(RING):
        if k:
            wait_in(fin.at[0, k], f_recv.at[k])
        wait_in(fin.at[1, k], f_recv.at[RING + k])
    for g in range(RING):
        fin_out[0, g] = fin[0, lax.rem(r + RING - g, RING)]
        fin_out[1, g] = fin[1, lax.rem(q + RING - g, RING)]

    for k in range(3):
        wait_in(att_out.at[r_from[k]], att_recv.at[k])
    for copy in sent:
        copy.wait_send()
    own_att.wait()


def results_kernel(att_ref, sums_ref, att_out, dw_out):
    for g in range(RING):
        att_out[:, g * QW:(g + 1) * QW] = att_ref[g]
        got = sums_ref[0, g].astype(F32) + sums_ref[1, g].astype(F32)
        dw_out[:, g * QW:(g + 1) * QW] = got[:, 0:QW]
        dw_out[:, 2048 + g * HD:2048 + (g + 1) * HD] = got[:, QW:QW + HD]
        dw_out[:, 2560 + g * HD:2560 + (g + 1) * HD] = got[:, QW + HD:GW]


def body(inputs, w_qkv, random_blocks, d_out):
    dma = pltpu.SemaphoreType.DMA
    vm = pltpu.VMEM
    hbm = pl.BlockSpec(memory_space=pltpu.HBM)
    attended, sums = pl.pallas_call(
        kernel,
        out_shape=[jax.ShapeDtypeStruct((RING, TOK, QW), BF), jax.ShapeDtypeStruct((2, RING, 16, GW), BF)],
        in_specs=[hbm, hbm, hbm, hbm],
        out_specs=[pl.BlockSpec(memory_space=pltpu.VMEM)] * 2,
        scratch_shapes=[
            pltpu.SMEM((NRAND, QBLOCKS), jnp.int32),
            dma(()),
            vm((TOK, D), BF),
            vm((D, RING * KV), BF),
            vm((RING, D, QW), BF),
            vm((3, TOK, QW), BF),
            vm((RING, 2, BLOCK, KV), BF),
            vm((3, TOK, QW), BF),
            vm((QBLOCKS, BLOCK, KV), BF),
            vm((RING, TOK, QW), BF),
            vm((RING, TOK, QW), BF),
            vm((RING, TOK, QW), BF),
            vm((RING, TOK, QW), BF),
            vm((QBLOCKS, BLOCK, KV), F32),
            vm((PICKS + 1, BLOCK, KV), F32),
            vm((8 * BLOCK, KV), BF),
            pltpu.SMEM((QBLOCKS,), jnp.int32),
            vm((RING, RING * RING, RING, 32, TOK), BF),
            vm((QBLOCKS, BLOCK, KV), BF),
            vm((2, RING, BLOCK, KV), BF),
            vm((2, LOCAL, BLOCK, KV), BF),
            vm((LOCAL, BLOCK, KV), BF),
            vm((4, RING, 128, QW), BF),
            vm((2, 2, 128, QW), BF),
            vm((2, RING, 128, QW), BF),
            vm((3, 128, QW), BF),
            vm((3, 128, QW), BF),
            vm((4, RING, 128, KV), BF),
            vm((3, RING, 128, KV), BF),
            vm((3, 128, KV), BF),
            vm((3, 128, KV), BF),
            vm((RING, 2, 16, GW), BF),
            vm((2, RING, 16, GW), BF),
            dma((4,)), dma((4,)), dma((4,)),
            dma((3,)), dma((3,)), dma((16,)), dma((16,)), dma((3,)), dma((3,)), dma((3,)), dma((3,)), dma((6,)), dma((6,)),
            dma((6,)), dma((6,)), dma((3,)), dma((3,)), dma((6,)), dma((6,)), dma((3,)), dma((3,)), dma((3,)), dma((3,)),
            dma((3,)), dma((3,)), dma((8,)), dma((8,)),
        ],
        compiler_params=pltpu.CompilerParams(collective_id=1, has_side_effects=True, vmem_limit_bytes=62 * 2**20),
        cost_estimate=pl.CostEstimate(flops=13 * 10**9, bytes_accessed=20 * 2**20, transcendentals=2**22),
        name="attention_weight_gradient",
    )(random_blocks.T, inputs[0], w_qkv, d_out[0])
    attended, d_wqkv = pl.pallas_call(
        results_kernel,
        out_shape=[jax.ShapeDtypeStruct((TOK, D), BF), jax.ShapeDtypeStruct((16, RING * GW), F32)],
        in_specs=[pl.BlockSpec(memory_space=pltpu.VMEM)] * 2,
        out_specs=[pl.BlockSpec(memory_space=pltpu.VMEM)] * 2,
        name="results",
    )(attended, sums)
    return attended[None], d_wqkv


def solution(mesh):
    return jax.shard_map(
        body,
        mesh=mesh,
        in_specs=(P("dp", "seq", None), P(), P(), P("dp", "seq", None)),
        out_specs=(P("dp", "seq", None), P(("seq", "dp"), None)),
        check_vma=False,
    )
```
